256 devices in a mesh: dp: 4 (over y), seq: 64 (over z, x, core).
Axes of the slice: x: 4, y: 4, z: 8, core: 2. Of those that a mesh axis runs over, the one named last changes fastest.
Arguments:
- queries: bfloat16 [4, 8192, 8192], P('dp', 'seq'), may hold values from -6 to 6
- keys: bfloat16 [4, 8192, 1024], P('dp', 'seq'), may hold values from -6 to 6
- values: bfloat16 [4, 8192, 1024], P('dp', 'seq'), may hold values from -6 to 6
- grad_out: bfloat16 [4, 8192, 8192], P('dp', 'seq'), may hold values from -6 to 6
- q_gain: float32 [64, 128], P('seq'), may hold values from 0.1 to 1.9
- k_gain: float32 [8, 128], replicated, may hold values from 0.1 to 1.9
- block_lists: int32 [4, 128, 8], P('dp'), may hold values from 0 to 127, as said below
Outputs:
- attended: bfloat16 [4, 8192, 8192], P('dp', 'seq')
- grad_queries: bfloat16 [4, 8192, 8192], P('dp', 'seq')
- grad_keys: bfloat16 [4, 8192, 1024], P('dp', 'seq')
- grad_values: bfloat16 [4, 8192, 1024], P('dp', 'seq')
- grad_q_gain: float32 [64, 128], P('seq')
- grad_k_gain: float32 [8, 128], replicated
The draws below stay inside these ranges and needn't reach their ends.
Inputs may be any that keep to these rules, and one draw needn't show every extreme that they name: `block_lists`: for query block i, slots 0 to 2 hold blocks i - 1 + s modulo 128, the next 2 slots hold blocks 0 to 1, the last 3 any blocks; entries may repeat.
All inputs are finite; a program needn't handle non-finite values.
Results may differ from the reference program's by a relative error of at most 0.0085.
Values may be sent and summed in bfloat16 or wider, within the bound.
A program may use at most 192 MiB of HBM per device.

```python
import math
import jax
import jax.numpy as jnp
from jax import lax

HEADS = 64
KV_HEADS = 8
HEAD_DIM = 128
BLOCK = 64
WINDOW = 3
GLOBALS = 2
RANDOMS = 3
SEQ = 8192
SEQS = 4
BLOCKS = 128


def draw_block_lists(key, part):
    key = jax.random.fold_in(key, 11)
    rows = jnp.arange(BLOCKS, dtype=jnp.int32)
    window_part = (rows[:, None] + jnp.arange(WINDOW, dtype=jnp.int32)[None, :] - WINDOW // 2) % BLOCKS
    window_part = jnp.broadcast_to(window_part[None], (SEQS, BLOCKS, WINDOW))
    global_part = jnp.broadcast_to(jnp.arange(GLOBALS, dtype=jnp.int32)[None, None, :], (SEQS, BLOCKS, GLOBALS))
    random_part = jax.random.randint(key, (SEQS, BLOCKS, RANDOMS), 0, BLOCKS, dtype=jnp.int32)
    return jnp.concatenate([window_part.astype(jnp.int32), global_part.astype(jnp.int32), random_part], axis=2)


def block_scale(rng, extent, shards, smallest, high):
    def one(dim, shards_of):
        draws = jax.random.uniform(jax.random.fold_in(jax.random.fold_in(rng, 6), dim), (shards_of,), jnp.float32, smallest / len(shards), high / len(shards))
        return jnp.repeat(jnp.exp(draws), extent[dim] // shards_of).reshape((-1,) + (1,) * (len(extent) - dim - 1))

    loudness = one(*shards[0])
    for cut in shards[1:]:
        loudness = loudness * one(*cut)
    return loudness


def bell_draw(rng, extent, spread, bound, shards=(), kind=jnp.bfloat16):
    factor_of = block_scale(rng, extent, shards, -0.22, 0.18) if shards else 1.0
    entries = jax.random.normal(rng, extent, jnp.float32) * spread * factor_of
    return jnp.minimum(jnp.maximum(entries, -bound), bound).astype(kind)


def setup_inputs(seed: int = 0) -> dict:
    key_of = jax.random.split(jax.random.key(seed), 8)
    queries = bell_draw(key_of[0], (SEQS, SEQ, HEADS * HEAD_DIM), 1.0, 6.0, ((0, 4), (1, 64)))
    keys = bell_draw(key_of[1], (SEQS, SEQ, KV_HEADS * HEAD_DIM), 1.0, 6.0, ((0, 4), (1, 64)))
    values = bell_draw(key_of[2], (SEQS, SEQ, KV_HEADS * HEAD_DIM), 1.0, 6.0, ((0, 4), (1, 64)))
    grad_out = bell_draw(key_of[3], (SEQS, SEQ, HEADS * HEAD_DIM), 1.0, 6.0, ((0, 4), (1, 64)))
    q_gain = jnp.clip(1.0 + 0.18 * jax.random.normal(key_of[4], (HEADS, HEAD_DIM), jnp.float32), 0.1, 1.9)
    k_gain = jnp.clip(1.0 + 0.18 * jax.random.normal(key_of[5], (KV_HEADS, HEAD_DIM), jnp.float32), 0.1, 1.9)
    block_lists = draw_block_lists(jax.random.fold_in(key_of[7], 71), 0)
    return dict(queries=queries, keys=keys, values=values, grad_out=grad_out, q_gain=q_gain, k_gain=k_gain, block_lists=block_lists)


EPSILON = 1e-06

def rounded(tensor):
    return lax.optimization_barrier(tensor.astype(jnp.bfloat16)).astype(jnp.float32)

def head_pass(query, key_head, value_head, out_grad, gain_q, gain_k, lists):
    score_scale = 1.0 / math.sqrt(HEAD_DIM)
    query_float = query.astype(jnp.float32)
    query_scale = lax.rsqrt(lax.optimization_barrier(jnp.mean(query_float * query_float, -1, keepdims=True)) + EPSILON)
    query_normed = rounded(query_float * query_scale * gain_q)
    key_float = key_head.astype(jnp.float32)
    key_scale = lax.rsqrt(lax.optimization_barrier(jnp.mean(key_float * key_float, -1, keepdims=True)) + EPSILON)
    key_normed = rounded(key_float * key_scale * gain_k)
    query_blocks = query_normed.reshape(BLOCKS, BLOCK, HEAD_DIM)
    key_blocks = key_normed.reshape(BLOCKS, BLOCK, HEAD_DIM)[lists]
    value_blocks = value_head.astype(jnp.float32).reshape(BLOCKS, BLOCK, HEAD_DIM)[lists]
    scores = jnp.einsum('nid,nkjd->nikj', query_blocks, key_blocks) * score_scale
    expo = jnp.exp(scores)
    probs = expo / lax.optimization_barrier(jnp.sum(expo, axis=(2, 3), keepdims=True))
    probs_low = rounded(probs)
    attended = jnp.einsum('nikj,nkjd->nid', probs_low, value_blocks)
    grad_blocks = out_grad.astype(jnp.float32).reshape(BLOCKS, BLOCK, HEAD_DIM)
    dprobs = jnp.einsum('nid,nkjd->nikj', grad_blocks, value_blocks)
    delta = lax.optimization_barrier(jnp.sum(probs * dprobs, axis=(2, 3), keepdims=True))
    dscores = rounded(probs * (dprobs - delta))
    dq_normed = (jnp.einsum('nikj,nkjd->nid', dscores, key_blocks) * score_scale).reshape(SEQ, HEAD_DIM)
    key_terms = jnp.einsum('nikj,nid->nkjd', dscores, query_blocks) * score_scale
    dk_normed = jnp.zeros((BLOCKS, BLOCK, HEAD_DIM), jnp.float32).at[lists].add(key_terms).reshape(SEQ, HEAD_DIM)
    value_terms = jnp.einsum('nikj,nid->nkjd', probs_low, grad_blocks)
    dv_head = jnp.zeros((BLOCKS, BLOCK, HEAD_DIM), jnp.float32).at[lists].add(value_terms).reshape(SEQ, HEAD_DIM)
    grad_query = query_scale * (gain_q * dq_normed - query_float * query_scale * query_scale * lax.optimization_barrier(jnp.mean(query_float * gain_q * dq_normed, -1, keepdims=True)))
    dk_head = key_scale * (gain_k * dk_normed - key_float * key_scale * key_scale * lax.optimization_barrier(jnp.mean(key_float * gain_k * dk_normed, -1, keepdims=True)))
    gain_q_grad = lax.optimization_barrier(jnp.sum(dq_normed * query_float * query_scale, 0))
    gain_k_grad = lax.optimization_barrier(jnp.sum(dk_normed * key_float * key_scale, 0))
    return (attended.reshape(SEQ, HEAD_DIM).astype(jnp.bfloat16), grad_query.astype(jnp.bfloat16), dk_head.astype(jnp.bfloat16), dv_head.astype(jnp.bfloat16), gain_q_grad, gain_k_grad)

def reference(queries, keys, values, grad_out, q_gain, k_gain, block_lists):
    group_size = HEADS // KV_HEADS
    outs_all, dq_all, dk_all, dv_all = ([], [], [], [])
    gain_q_total = jnp.zeros((HEADS, HEAD_DIM), jnp.float32)
    gain_k_total = jnp.zeros((KV_HEADS, HEAD_DIM), jnp.float32)
    gain_k_wide = jnp.repeat(k_gain, group_size, 0)
    for seq_id in range(SEQS):
        query_heads = queries[seq_id].reshape(SEQ, HEADS, HEAD_DIM).transpose(1, 0, 2)
        grad_heads = grad_out[seq_id].reshape(SEQ, HEADS, HEAD_DIM).transpose(1, 0, 2)
        key_heads = jnp.repeat(keys[seq_id].reshape(SEQ, KV_HEADS, HEAD_DIM).transpose(1, 0, 2), group_size, 0)
        value_heads = jnp.repeat(values[seq_id].reshape(SEQ, KV_HEADS, HEAD_DIM).transpose(1, 0, 2), group_size, 0)
        lists = block_lists[seq_id]
        results = lax.map(lambda items: head_pass(*items, lists), (query_heads, key_heads, value_heads, grad_heads, q_gain, gain_k_wide))
        attended, grad_query, dk_head, dv_head, gain_q_grad, gain_k_grad = results
        outs_all.append(attended.transpose(1, 0, 2).reshape(SEQ, HEADS * HEAD_DIM))
        dq_all.append(grad_query.transpose(1, 0, 2).reshape(SEQ, HEADS * HEAD_DIM))
        dk_sum = lax.optimization_barrier(jnp.sum(dk_head.astype(jnp.float32).reshape(KV_HEADS, group_size, SEQ, HEAD_DIM), 1))
        dv_sum = lax.optimization_barrier(jnp.sum(dv_head.astype(jnp.float32).reshape(KV_HEADS, group_size, SEQ, HEAD_DIM), 1))
        dk_all.append(dk_sum.astype(jnp.bfloat16).transpose(1, 0, 2).reshape(SEQ, KV_HEADS * HEAD_DIM))
        dv_all.append(dv_sum.astype(jnp.bfloat16).transpose(1, 0, 2).reshape(SEQ, KV_HEADS * HEAD_DIM))
        gain_q_total = gain_q_total + gain_q_grad
        gain_k_total = gain_k_total + lax.optimization_barrier(jnp.sum(gain_k_grad.reshape(KV_HEADS, group_size, HEAD_DIM), 1))
    return (jnp.stack(outs_all), jnp.stack(dq_all), jnp.stack(dk_all), jnp.stack(dv_all), gain_q_total, gain_k_total)
```

```python
import functools
import math

import jax
import jax.numpy as jnp
from jax import lax
from jax.experimental import pallas as pl
from jax.experimental.pallas import tpu as pltpu
from jax.sharding import PartitionSpec as P

EPSILON = 1e-06
BLOCK = 64
SUBS = 2
MESH = pl.DeviceIdType.MESH
ANY = pl.BlockSpec(memory_space=pl.ANY)
VMEM = pl.BlockSpec(memory_space=pltpu.VMEM)
LIMIT = 56 * 1024 * 1024


def place(cols):
    seq = lax.axis_index("seq")
    return lax.axis_index("dp"), seq // cols, seq % cols


def greet(devices):
    barrier = pltpu.get_barrier_semaphore()
    for device in devices:
        pl.semaphore_signal(barrier, inc=1, device_id=device, device_id_type=MESH)
    pl.semaphore_wait(barrier, len(devices))


def push(src, dst, send_sem, recv_sem, device):
    copy = pltpu.make_async_remote_copy(
        src_ref=src,
        dst_ref=dst,
        send_sem=send_sem,
        recv_sem=recv_sem,
        device_id=device,
        device_id_type=MESH,
    )
    copy.start()
    return copy


def move(src, dst, sem):
    copy = pltpu.make_async_copy(src, dst, sem)
    copy.start()
    return copy


def aligned(index, size):
    return pl.ds(pl.multiple_of(index * size, size), size)


def gather_kernel(
    rows,
    cols,
    q_ref,
    go_ref,
    k_ref,
    v_ref,
    qg_ref,
    kg_ref,
    qh_ref,
    goh_ref,
    kall_ref,
    vall_ref,
    gq_ref,
    kx,
    vx,
    kn,
    gain,
    gx,
    gz,
    own_sem,
    wide_send,
    wide_recv,
    kv_send,
    kv_recv,
    gx_send,
    gx_recv,
    k_send,
    k_recv,
    v_send,
    v_recv,
    gz_send,
    gz_recv,
):
    dp, z, c = place(cols)
    tok = q_ref.shape[0]
    width = q_ref.shape[1] // cols
    head = k_ref.shape[1] // cols

    def at(zz, cc):
        return (dp, lax.rem(zz, rows) * cols + lax.rem(cc, cols))

    right, left = at(z + 1, c), at(z + rows - 1, c)
    partners = {d: at(z, c + d) for d in range(1, cols)}
    gain[...] = jnp.broadcast_to(qg_ref[...], gain.shape)
    greet(list(partners.values()) + [right, left])

    mine = aligned(c, tok)
    small, large, local = [], [], []
    for d in range(1, cols):
        part = aligned(lax.rem(c + d, cols), head)
        for i, (src, dst) in enumerate(((k_ref, kx), (v_ref, vx))):
            small.append(
                push(src.at[:, part], dst.at[mine, :], kv_send.at[i, d], kv_recv.at[i, d], partners[d])
            )
        small.append(push(gain, gx.at[c], gx_send.at[d], gx_recv.at[d], partners[d]))
    own = [
        move(src.at[:, aligned(c, head)], dst.at[mine, :], own_sem.at[i])
        for i, (src, dst) in enumerate(((k_ref, kx), (v_ref, vx)))
    ]
    for d in range(1, cols):
        part = aligned(lax.rem(c + d, cols), width)
        for i, (src, dst) in enumerate(((q_ref, qh_ref), (go_ref, goh_ref))):
            large.append(
                push(src.at[:, part], dst.at[mine, :], wide_send.at[i, d], wide_recv.at[i, d], partners[d])
            )
    for i, (src, dst) in enumerate(((q_ref, qh_ref), (go_ref, goh_ref))):
        local.append(move(src.at[:, aligned(c, width)], dst.at[mine, :], own_sem.at[2 + i]))

    for copy in own + small:
        copy.wait()
    key = kx[...].astype(jnp.float32)
    scale = lax.rsqrt(jnp.mean(key * key, -1, keepdims=True) + EPSILON)
    kn[...] = (key * scale * kg_ref[pl.ds(c, 1), :]).astype(jnp.bfloat16)
    gx[c] = gain[...]
    gz[z] = jnp.concatenate([gx[i, :1, :] for i in range(cols)], axis=0)
    local.append(move(kn, kall_ref.at[z], own_sem.at[4]))
    local.append(move(vx, vall_ref.at[z], own_sem.at[5]))

    sub = kn.shape[0] // SUBS
    ring = {}
    for t in range(rows - 1):
        k_slot, v_slot = lax.rem(z + rows - t, rows), lax.rem(z + t, rows)
        for s in range(SUBS):
            part = pl.ds(s * sub, sub)
            k_dst, v_dst = kall_ref.at[k_slot, part, :], vall_ref.at[v_slot, part, :]
            if t:
                ring["k", t - 1, s].wait_recv()
            k_src = k_dst if t else kn.at[part, :]
            ring["k", t, s] = push(k_src, k_dst, k_send.at[t, s], k_recv.at[t, s], right)
            if t:
                ring["v", t - 1, s].wait_recv()
            v_src = v_dst if t else vx.at[part, :]
            ring["v", t, s] = push(v_src, v_dst, v_send.at[t, s], v_recv.at[t, s], left)
        if t:
            ring["g", t - 1, 0].wait_recv()
        ring["g", t, 0] = push(gz.at[k_slot], gz.at[k_slot], gz_send.at[t], gz_recv.at[t], right)
    for (_, t, _), copy in ring.items():
        if t == rows - 2:
            copy.wait_recv()
        copy.wait_send()
    gq_ref[...] = gz[c]
    for copy in local + large:
        copy.wait()


def gather(rows, cols, queries, grad_out, keys, values, q_gain, k_gain):
    tok, wide = queries.shape
    head = keys.shape[1] // cols
    group = cols * tok
    sem = pltpu.SemaphoreType.DMA
    low = jnp.bfloat16
    return pl.pallas_call(
        functools.partial(gather_kernel, rows, cols),
        out_shape=(
            jax.ShapeDtypeStruct((group, wide // cols), low),
            jax.ShapeDtypeStruct((group, wide // cols), low),
            jax.ShapeDtypeStruct((rows, group, head), low),
            jax.ShapeDtypeStruct((rows, group, head), low),
            jax.ShapeDtypeStruct((cols, head), jnp.float32),
        ),
        in_specs=[ANY] * 4 + [VMEM] * 2,
        out_specs=(ANY, ANY, ANY, ANY, VMEM),
        scratch_shapes=[
            pltpu.VMEM((group, head), low),
            pltpu.VMEM((group, head), low),
            pltpu.VMEM((group, head), low),
            pltpu.VMEM((8, head), jnp.float32),
            pltpu.VMEM((cols, 8, head), jnp.float32),
            pltpu.VMEM((rows, cols, head), jnp.float32),
            sem((6,)),
            sem((2, cols)),
            sem((2, cols)),
            sem((2, cols)),
            sem((2, cols)),
            sem((cols,)),
            sem((cols,)),
            sem((rows, SUBS)),
            sem((rows, SUBS)),
            sem((rows, SUBS)),
            sem((rows, SUBS)),
            sem((rows,)),
            sem((rows,)),
        ],
        compiler_params=pltpu.CompilerParams(
            collective_id=0, has_side_effects=True, vmem_limit_bytes=LIMIT
        ),
        cost_estimate=pl.CostEstimate(flops=0, bytes_accessed=16 << 20, transcendentals=0),
    )(queries, grad_out, keys, values, q_gain, k_gain)


def dot(a, b, dims):
    return lax.dot_general(a, b, (dims, ((), ())), preferred_element_type=jnp.float32)


def attend_kernel(
    cols,
    steps,
    slots,
    lists_ref,
    q_ref,
    go_ref,
    k_ref,
    v_ref,
    gq_ref,
    kg_ref,
    a_ref,
    dq_ref,
    dk_ref,
    dv_ref,
    gp_ref,
    dk_acc,
    dv_acc,
    gq_acc,
):
    n = pl.program_id(0)
    _, z, c = place(cols)
    head = k_ref.shape[1]
    heads = q_ref.shape[1] // head
    score_scale = 1.0 / math.sqrt(head)

    @pl.when(n == 0)
    def _():
        dk_acc[...] = jnp.zeros_like(dk_acc)
        dv_acc[...] = jnp.zeros_like(dv_acc)
        gq_acc[...] = jnp.zeros_like(gq_acc)

    ids = [lists_ref[(z * steps + n) * slots + s] for s in range(slots)]
    spans = [aligned(i, BLOCK) for i in ids]
    key = jnp.concatenate([k_ref[span, :] for span in spans], axis=0)
    value = jnp.concatenate([v_ref[span, :] for span in spans], axis=0)
    cut = [slice(h * head, (h + 1) * head) for h in range(heads)]
    raw = [q_ref[:, s].astype(jnp.float32) for s in cut]
    scales = [lax.rsqrt(jnp.mean(x * x, -1, keepdims=True) + EPSILON) for x in raw]
    normed = jnp.concatenate(
        [(x * s * gq_ref[h : h + 1, :]).astype(jnp.bfloat16) for h, (x, s) in enumerate(zip(raw, scales))],
        axis=0,
    )
    grad = jnp.concatenate([go_ref[:, s] for s in cut], axis=0)

    scores = dot(key, normed, ((1,), (1,)))
    expo = jnp.exp2(scores * (score_scale * math.log2(math.e)))
    probs = expo * (1.0 / jnp.sum(expo, axis=0, keepdims=True))
    low = probs.astype(jnp.bfloat16)
    out = dot(value, low, ((0,), (0,))).T
    dprobs = dot(value, grad, ((1,), (1,)))
    delta = jnp.sum(probs * dprobs, axis=0, keepdims=True)
    dscores = (probs * (dprobs - delta)).astype(jnp.bfloat16)
    dq = dot(key, dscores, ((0,), (0,))).T * score_scale
    dk = dot(dscores, normed, ((1,), (0,)))
    dv = dot(low, grad, ((1,), (0,)))
    for s, span in enumerate(spans):
        part = slice(s * BLOCK, (s + 1) * BLOCK)
        dk_acc[span, :] += dk[part]
        dv_acc[span, :] += dv[part]
    for h in range(heads):
        part = slice(h * BLOCK, (h + 1) * BLOCK)
        a_ref[:, cut[h]] = out[part].astype(jnp.bfloat16)
        x, s, d = raw[h], scales[h], dq[part]
        gain = gq_ref[h : h + 1, :]
        unit = x * s
        gq_acc[h : h + 1, :] += jnp.sum(d * unit, 0, keepdims=True)
        gd = gain * d
        dq_ref[:, cut[h]] = (s * (gd - unit * jnp.mean(unit * gd, -1, keepdims=True))).astype(jnp.bfloat16)

    @pl.when(n == steps - 1)
    def _():
        chunk = 512

        def finish(i, total):
            span = pl.ds(pl.multiple_of(i * chunk, chunk), chunk)
            d = dk_acc[span, :] * score_scale
            dk_ref[span, :] = d.astype(jnp.bfloat16)
            dv_ref[span, :] = dv_acc[span, :].astype(jnp.bfloat16)
            return total + jnp.sum(d * k_ref[span, :].astype(jnp.float32), 0, keepdims=True)

        total = lax.fori_loop(0, dk_acc.shape[0] // chunk, finish, jnp.zeros((1, head), jnp.float32))
        gp_ref[:heads, :] = gq_acc[...]
        gp_ref[heads:, :] = jnp.broadcast_to(total / kg_ref[pl.ds(c, 1), :], (heads, head))


def attend(cols, lists, q, go, k, v, gq, k_gain):
    group, width = q.shape
    tokens, head = k.shape
    heads = width // head
    steps = group // BLOCK
    slots = lists.shape[1]
    step_spec = pl.BlockSpec((BLOCK, width), lambda n, _: (n, 0))
    low = jnp.bfloat16
    flops = 6 * 2 * group * heads * slots * BLOCK * head
    return pl.pallas_call(
        functools.partial(attend_kernel, cols, steps, slots),
        grid_spec=pltpu.PrefetchScalarGridSpec(
            num_scalar_prefetch=1,
            grid=(steps,),
            in_specs=[step_spec, step_spec] + [VMEM] * 4,
            out_specs=(step_spec, step_spec, VMEM, VMEM, VMEM),
            scratch_shapes=[
                pltpu.VMEM((tokens, head), jnp.float32),
                pltpu.VMEM((tokens, head), jnp.float32),
                pltpu.VMEM((heads, head), jnp.float32),
            ],
        ),
        out_shape=(
            jax.ShapeDtypeStruct((group, width), low),
            jax.ShapeDtypeStruct((group, width), low),
            jax.ShapeDtypeStruct((tokens, head), low),
            jax.ShapeDtypeStruct((tokens, head), low),
            jax.ShapeDtypeStruct((2 * heads, head), jnp.float32),
        ),
        compiler_params=pltpu.CompilerParams(vmem_limit_bytes=LIMIT),
        cost_estimate=pl.CostEstimate(flops=flops, bytes_accessed=16 << 20, transcendentals=0),
    )(lists.reshape(-1), q, go, k, v, gq, k_gain)


def scatter_kernel(
    rows,
    cols,
    depth,
    a_ref,
    dq_ref,
    dk_ref,
    dv_ref,
    gp_ref,
    k_ref,
    kg_ref,
    a_out,
    dq_out,
    dk_out,
    dv_out,
    gq_out,
    gk_out,
    k_sum,
    v_sum,
    k_fin,
    v_fin,
    k_land,
    v_land,
    g1,
    g2,
    g3,
    own_sem,
    wide_send,
    wide_recv,
    k_send,
    k_recv,
    v_send,
    v_recv,
    kv_send,
    kv_recv,
    g1_send,
    g1_recv,
    g2_send,
    g2_recv,
    g3_send,
    g3_recv,
):
    dp, z, c = place(cols)
    tok, head = k_ref.shape[0], k_ref.shape[1] // cols
    width = a_ref.shape[1]

    def at(zz, cc):
        return (dp, lax.rem(zz, rows) * cols + lax.rem(cc, cols))

    across = {d: at(z, c + d) for d in range(1, cols)}
    along = {d: at(z + d, c) for d in range(1, rows)}
    over = {d: (lax.rem(dp + d, depth), z * cols + c) for d in range(1, depth)}
    right, left = along[1], along[rows - 1]
    greet(list(across.values()) + list(along.values()) + list(over.values()))

    sub = k_sum.shape[1] // SUBS
    mine = aligned(c, width)
    large, gains = [], []
    ring = {}

    def ring_step(t):
        k_chunk = lax.rem(z + 2 * rows - 1 - t, rows)
        v_chunk = lax.rem(z + 1 + t, rows)
        for s in range(SUBS):
            part = pl.ds(s * sub, sub)
            for name, chunk, ref, sums, send, recv, to in (
                ("k", k_chunk, dk_ref, k_sum, k_send, k_recv, right),
                ("v", v_chunk, dv_ref, v_sum, v_send, v_recv, left),
            ):
                src = ref.at[chunk, part, :]
                if t:
                    ring[name, t - 1, s].wait_recv()
                    src = sums.at[t - 1, part, :]
                    total = src[...].astype(jnp.float32) + ref[chunk, part, :].astype(jnp.float32)
                    src[...] = total.astype(jnp.bfloat16)
                ring[name, t, s] = push(src, sums.at[t, part, :], send.at[t, s], recv.at[t, s], to)

    ring_step(0)
    for d in range(1, cols):
        part = aligned(lax.rem(c + d, cols), tok)
        for i, (src, dst) in enumerate(((a_ref, a_out), (dq_ref, dq_out))):
            large.append(
                push(src.at[part, :], dst.at[:, mine], wide_send.at[i, d], wide_recv.at[i, d], across[d])
            )
    for i, (src, dst) in enumerate(((a_ref, a_out), (dq_ref, dq_out))):
        large.append(move(src.at[aligned(c, tok), :], dst.at[:, mine], own_sem.at[i]))

    one = [push(gp_ref, g1.at[z], g1_send.at[d], g1_recv.at[d], along[d]) for d in range(1, rows)]
    ring_step(1)
    for copy in one:
        copy.wait()
    g1[z] = gp_ref[...]
    g2[dp] = jnp.sum(g1[...], 0)
    two = [push(g2.at[dp], g2.at[dp], g2_send.at[d], g2_recv.at[d], over[d]) for d in range(1, depth)]
    ring_step(2)
    for copy in two:
        copy.wait()
    g3[c] = jnp.sum(g2[...], 0)
    three = [push(g3.at[c], g3.at[c], g3_send.at[d], g3_recv.at[d], across[d]) for d in range(1, cols)]
    for t in range(3, rows - 1):
        ring_step(t)
    for copy in three:
        copy.wait()
    gq_out[...] = g3[z, pl.ds(c, 1), :]
    gk_out[...] = jnp.concatenate([g3[i, cols : cols + 1, :] for i in range(cols)], axis=0)

    last = rows - 2
    for s in range(SUBS):
        part = pl.ds(s * sub, sub)
        for name, ref, sums, fin in (("k", dk_ref, k_sum, k_fin), ("v", dv_ref, v_sum, v_fin)):
            ring[name, last, s].wait_recv()
            total = sums[last, part, :].astype(jnp.float32) + ref[z, part, :].astype(jnp.float32)
            fin[part, :] = total.astype(jnp.bfloat16)
    back = []
    for d in range(1, cols):
        part = aligned(lax.rem(c + d, cols), tok)
        for i, (fin, land) in enumerate(((k_fin, k_land), (v_fin, v_land))):
            back.append(push(fin.at[part, :], land.at[c], kv_send.at[i, d], kv_recv.at[i, d], across[d]))
    for copy in back:
        copy.wait()
    k_land[c] = k_fin[aligned(c, tok), :]
    v_land[c] = v_fin[aligned(c, tok), :]
    for i in range(cols):
        cut = slice(i * head, (i + 1) * head)
        raw = k_ref[:, cut].astype(jnp.float32)
        scale = lax.rsqrt(jnp.mean(raw * raw, -1, keepdims=True) + EPSILON)
        unit = raw * scale
        gd = kg_ref[i : i + 1, :] * k_land[i].astype(jnp.float32)
        dk_out[:, cut] = (scale * (gd - unit * jnp.mean(unit * gd, -1, keepdims=True))).astype(jnp.bfloat16)
        dv_out[:, cut] = v_land[i]
    for copy in ring.values():
        copy.wait_send()
    for copy in large:
        copy.wait()


def scatter(rows, cols, depth, a, dq, dk, dv, gp, keys, k_gain):
    tok = keys.shape[0]
    head = keys.shape[1] // cols
    group, width = a.shape
    sem = pltpu.SemaphoreType.DMA
    low = jnp.bfloat16
    return pl.pallas_call(
        functools.partial(scatter_kernel, rows, cols, depth),
        out_shape=(
            jax.ShapeDtypeStruct((tok, width * cols), low),
            jax.ShapeDtypeStruct((tok, width * cols), low),
            jax.ShapeDtypeStruct((tok, head * cols), low),
            jax.ShapeDtypeStruct((tok, head * cols), low),
            jax.ShapeDtypeStruct((1, head), jnp.float32),
            jax.ShapeDtypeStruct((cols, head), jnp.float32),
        ),
        in_specs=[ANY] * 2 + [VMEM] * 5,
        out_specs=(ANY, ANY, VMEM, VMEM, VMEM, VMEM),
        scratch_shapes=[
            pltpu.VMEM((rows - 1, group, head), low),
            pltpu.VMEM((rows - 1, group, head), low),
            pltpu.VMEM((group, head), low),
            pltpu.VMEM((group, head), low),
            pltpu.VMEM((cols, tok, head), low),
            pltpu.VMEM((cols, tok, head), low),
            pltpu.VMEM((rows, 2 * cols, head), jnp.float32),
            pltpu.VMEM((depth, 2 * cols, head), jnp.float32),
            pltpu.VMEM((cols, 2 * cols, head), jnp.float32),
            sem((2,)),
            sem((2, cols)),
            sem((2, cols)),
            sem((rows, SUBS)),
            sem((rows, SUBS)),
            sem((rows, SUBS)),
            sem((rows, SUBS)),
            sem((2, cols)),
            sem((2, cols)),
            sem((rows,)),
            sem((rows,)),
            sem((depth,)),
            sem((depth,)),
            sem((cols,)),
            sem((cols,)),
        ],
        compiler_params=pltpu.CompilerParams(
            collective_id=1, has_side_effects=True, vmem_limit_bytes=LIMIT
        ),
        cost_estimate=pl.CostEstimate(flops=0, bytes_accessed=16 << 20, transcendentals=0),
    )(a, dq, dk.reshape(rows, group, head), dv.reshape(rows, group, head), gp, keys, k_gain)


def on_device(depth, queries, keys, values, grad_out, q_gain, k_gain, block_lists):
    cols = k_gain.shape[0]
    rows = lax.axis_size("seq") // cols
    q, go, k, v, gq = gather(rows, cols, queries[0], grad_out[0], keys[0], values[0], q_gain, k_gain)
    head = k.shape[2]
    a, dq, dk, dv, gp = attend(
        cols, block_lists[0], q, go, k.reshape(-1, head), v.reshape(-1, head), gq, k_gain
    )
    a, dq, dk, dv, gain_q, gain_k = scatter(rows, cols, depth, a, dq, dk, dv, gp, keys[0], k_gain)
    return a[None], dq[None], dk[None], dv[None], gain_q, gain_k


def solution(mesh):
    spec = P("dp", "seq", None)
    return jax.shard_map(
        functools.partial(on_device, mesh.shape["dp"]),
        mesh=mesh,
        in_specs=(spec, spec, spec, spec, P("seq", None), P(), P("dp", None, None)),
        out_specs=(spec, spec, spec, spec, P("seq", None), P()),
        check_vma=False,
    )
```

```python
import functools
import math

import jax
import jax.numpy as jnp
from jax import lax
from jax.experimental import pallas as pl
from jax.experimental.pallas import tpu as pltpu
from jax.sharding import PartitionSpec as P

EPSILON = 1e-06
BLOCK = 64
SUBS = 2
MESH = pl.DeviceIdType.MESH
ANY = pl.BlockSpec(memory_space=pl.ANY)
VMEM = pl.BlockSpec(memory_space=pltpu.VMEM)
LIMIT = 60 * 1024 * 1024
WINDOW, GLOBALS = 3, 2


def place(cols):
    seq = lax.axis_index("seq")
    return lax.axis_index("dp"), seq // cols, seq % cols


def greet(devices):
    barrier = pltpu.get_barrier_semaphore()
    for device in devices:
        pl.semaphore_signal(barrier, inc=1, device_id=device, device_id_type=MESH)
    pl.semaphore_wait(barrier, len(devices))


def wire(src, dst, send_sem, recv_sem, device):
    return pltpu.make_async_remote_copy(
        src_ref=src,
        dst_ref=dst,
        send_sem=send_sem,
        recv_sem=recv_sem,
        device_id=device,
        device_id_type=MESH,
    )


def push(*args):
    copy = wire(*args)
    copy.start()
    return copy


def move(src, dst, sem):
    copy = pltpu.make_async_copy(src, dst, sem)
    copy.start()
    return copy


def aligned(index, size):
    return pl.ds(pl.multiple_of(index * size, size), size)


def dot(a, b, dims):
    return lax.dot_general(a, b, (dims, ((), ())), preferred_element_type=jnp.float32)


def kernel(
    rows,
    cols,
    depth,
    randoms,
    table,
    q_ref,
    go_ref,
    k_ref,
    v_ref,
    key_ref,
    qg_ref,
    kg_ref,
    a_out,
    dq_out,
    dk_out,
    dv_out,
    gq_out,
    gk_out,
    qx,
    gox,
    kx,
    kall,
    vall,
    gain,
    gx,
    gz,
    qn,
    probs,
    dk_base,
    dv_base,
    dk_rand,
    dv_rand,
    gq_acc,
    gk_acc,
    ax,
    dqx,
    k_sum,
    v_sum,
    k_fin,
    v_fin,
    k_land,
    v_land,
    g1,
    g2,
    g3,
    own_sem,
    in_send,
    in_recv,
    kv_send,
    kv_recv,
    gx_send,
    gx_recv,
    k_send,
    k_recv,
    v_send,
    v_recv,
    gz_send,
    gz_recv,
    out_send,
    out_recv,
    dk_send,
    dk_recv,
    dv_send,
    dv_recv,
    back_send,
    back_recv,
    g1_send,
    g1_recv,
    g2_send,
    g2_recv,
    g3_send,
    g3_recv,
):
    dp, z, c = place(cols)
    tok = q_ref.shape[0]
    width = q_ref.shape[1] // cols
    head = k_ref.shape[1] // cols
    heads = width // head
    group = cols * tok
    per = tok // BLOCK
    steps = group // BLOCK
    blocks = rows * steps
    sub = group // (2 * SUBS)
    score_scale = 1.0 / math.sqrt(head)
    low = jnp.bfloat16
    first_prev, first_last = steps * randoms, 2 * steps * randoms

    def at(zz, cc):
        return (dp, lax.rem(zz, rows) * cols + lax.rem(cc, cols))

    across = {d: at(z, c + d) for d in range(1, cols)}
    along = {d: at(z + d, c) for d in range(1, rows)}
    over = {d: (lax.rem(dp + d, depth), z * cols + c) for d in range(1, depth)}
    right, left = along[1], along[rows - 1]
    mine = aligned(c, tok)
    mine_wide = aligned(c, width)
    parts = [(h, s, h * SUBS + s) for s in range(SUBS) for h in range(2)]

    gain[...] = jnp.broadcast_to(qg_ref[...], gain.shape)
    greet(list(across.values()) + list(along.values()) + list(over.values()))

    small, local = [], []
    for d in range(1, cols):
        part = aligned(lax.rem(c + d, cols), head)
        small.append(push(k_ref.at[:, part], kx.at[mine, :], kv_send.at[0, d], kv_recv.at[0, d], across[d]))
        small.append(push(gain, gx.at[c], gx_send.at[d], gx_recv.at[d], across[d]))
    own_blocks = pl.ds(z * steps + c * per, per)
    late = []
    for d in range(1, cols):
        part = aligned(lax.rem(c + d, cols), head)
        late.append(push(v_ref.at[:, :, part], vall.at[own_blocks], kv_send.at[1, d], kv_recv.at[1, d], across[d]))
    own_k = move(k_ref.at[:, aligned(c, head)], kx.at[mine, :], own_sem.at[0])
    own_v = move(v_ref.at[:, :, aligned(c, head)], vall.at[own_blocks], own_sem.at[1])

    def bring(i, src, dst, d):
        part = aligned(lax.rem(c + d, cols), width)
        return push(src.at[:, part], dst.at[mine, :], in_send.at[i, d], in_recv.at[i, d], across[d])

    q_in = [bring(0, q_ref, qx, d) for d in range(1, cols)]
    own_q = move(q_ref.at[:, mine_wide], qx.at[mine, :], own_sem.at[2])
    own_go = move(go_ref.at[:, mine_wide], gox.at[mine, :], own_sem.at[3])
    for ref in (dk_base, dv_base, gq_acc, gk_acc):
        ref[...] = jnp.zeros_like(ref)
    for ref in (dk_rand, dv_rand, k_sum, v_sum):
        ref[0] = jnp.zeros(ref.shape[1:], ref.dtype)

    own_k.wait()
    for copy in small:
        copy.wait()
    raw_key = kx[...].astype(jnp.float32)
    scale = lax.rsqrt(jnp.mean(raw_key * raw_key, -1, keepdims=True) + EPSILON)
    normed_key = (raw_key * scale * kg_ref[pl.ds(c, 1), :]).astype(low)
    kall[pl.ds(z * steps, steps)] = normed_key.reshape(steps, BLOCK, head)
    gx[c] = gain[...]
    gz[z] = jnp.concatenate([gx[i, :1, :] for i in range(cols)], axis=0)

    def gather(ref, send, recv, t, h, i):
        slot = lax.rem(z + t, rows) if h else lax.rem(z + rows - t, rows)
        part = pl.ds(slot * steps + i * (sub // BLOCK), sub // BLOCK)
        return wire(ref.at[part], ref.at[part], send.at[t, i], recv.at[t, i], left if h else right)

    def gather_step(ref, send, recv, t, waits=True):
        for h, _, i in parts:
            if waits:
                gather(ref, send, recv, t - 1, h, i).wait_recv()
            gather(ref, send, recv, t, h, i).start()

    k_ring, v_ring = (kall, k_send, k_recv), (vall, v_send, v_recv)

    def gain_copy(t):
        slot = lax.rem(z + rows - t, rows)
        return wire(gz.at[slot], gz.at[slot], gz_send.at[t], gz_recv.at[t], right)

    lag = rows // 2
    go_in = []
    for t in range(rows - 1):
        gather_step(*k_ring, t, t > 0)
        if t:
            gain_copy(t - 1).wait_recv()
        gain_copy(t).start()
        if t == 1:
            own_v.wait()
            for copy in late:
                copy.wait()
        if t >= lag:
            gather_step(*v_ring, t - lag, t > lag)
            more = -(-(cols - 1) // (rows - 1 - lag))
            for d in range(cols - 1, 0, -1)[(t - lag) * more : (t - lag + 1) * more]:
                go_in.append(bring(1, go_ref, gox, d))
    for h, _, i in parts:
        gather(*k_ring, rows - 2, h, i).wait_recv()
    gain_copy(rows - 2).wait_recv()
    own_q.wait()
    for copy in q_in:
        copy.wait()

    cut = [slice(h * head, (h + 1) * head) for h in range(heads)]
    gains = [gz[c, h : h + 1, :] for h in range(heads)]

    def block_of(i):
        return lax.rem(per * (c + 1) + i, steps)

    def fixed(n):
        return [lax.rem(z * steps + n + s + blocks - WINDOW // 2, blocks) for s in range(WINDOW)] + list(range(GLOBALS))

    def listed(ref, i, n):
        ids = fixed(n) + [table[i * randoms + s] for s in range(randoms)]
        return jnp.concatenate([ref[b] for b in ids], axis=0)

    def unit_queries(n):
        raw = [qx[aligned(n, BLOCK), s].astype(jnp.float32) for s in cut]
        scales = [lax.rsqrt(jnp.mean(x * x, -1, keepdims=True) + EPSILON) for x in raw]
        return [x * s for x, s in zip(raw, scales)], scales

    def cotangents(n):
        return jnp.concatenate([gox[aligned(n, BLOCK), s] for s in cut], axis=0)

    def spread(base, rand, i, n, terms):
        for s, b in enumerate(fixed(n)):
            base[aligned(b, BLOCK), :] += terms[s * BLOCK : (s + 1) * BLOCK]
        for s in range(randoms):
            m = i * randoms + s
            first = (WINDOW + GLOBALS + s) * BLOCK
            rand[m + 1] = rand[table[first_prev + m]] + terms[first : first + BLOCK]

    def make_probs(i):
        n = block_of(i)
        units, _ = unit_queries(n)
        normed = jnp.concatenate([(u * g).astype(low) for u, g in zip(units, gains)], axis=0)
        qn[n] = normed
        scores = dot(normed, listed(kall, i, n), ((1,), (1,)))
        expo = jnp.exp2(scores * (score_scale * math.log2(math.e)))
        probs[n] = (expo * (1.0 / jnp.sum(expo, axis=1, keepdims=True))).astype(low)

    def make_dv(i):
        n = block_of(i)
        spread(dv_base, dv_rand, i, n, dot(probs[n], cotangents(n), ((0,), (0,))))

    def make_rest(i):
        n = block_of(i)
        key, value, grad, prob = listed(kall, i, n), listed(vall, i, n), cotangents(n), probs[n]
        out = dot(prob, value, ((1,), (0,)))
        dprobs = dot(grad, value, ((1,), (1,)))
        delta = jnp.sum(out * grad.astype(jnp.float32), axis=1, keepdims=True)
        dscores = (prob.astype(jnp.float32) * (dprobs - delta)).astype(low)
        dq = dot(dscores, key, ((1,), (0,))) * score_scale
        dk = dot(dscores, qn[n], ((0,), (0,))) * score_scale
        spread(dk_base, dk_rand, i, n, dk)
        gk_acc[...] += jnp.sum(dk * key.astype(jnp.float32), axis=0, keepdims=True)
        units, scales = unit_queries(n)
        for h in range(heads):
            part = slice(h * BLOCK, (h + 1) * BLOCK)
            ax[aligned(n, BLOCK), cut[h]] = out[part].astype(low)
            d, unit = dq[part], units[h]
            gq_acc[h : h + 1, :] += jnp.sum(d * unit, 0, keepdims=True)
            gd = gains[h] * d
            dqx[aligned(n, BLOCK), cut[h]] = (
                scales[h] * (gd - unit * jnp.mean(unit * gd, -1, keepdims=True))
            ).astype(low)

    def pair(work, j):
        for p in range(per):
            work(j * per + p)

    early = rows - 1 - lag
    share = cols // (rows - 1 - early)

    def probs_step(u, _):
        gather_step(*v_ring, u + early)
        for w in range(share):
            pair(make_probs, u * share + w)
        return 0

    lax.fori_loop(0, rows - 1 - early, probs_step, 0)

    own_go.wait()
    for copy in go_in:
        copy.wait()

    def dv_step(j, _):
        pair(make_dv, j)
        return 0

    lax.fori_loop(0, cols, dv_step, 0)
    for h, _, i in parts:
        gather(*v_ring, rows - 2, h, i).wait_recv()

    def reduce(sums, send, recv, t, h, i):
        part = pl.ds(i * sub, sub)
        return wire(sums.at[t, part, :], sums.at[t + 1, part, :], send.at[t, i], recv.at[t, i], left if h else right)

    def own_part(base, rand, chunk, i):
        start = chunk * group + i * sub
        return jnp.concatenate(
            [
                base[pl.ds(pl.multiple_of(start + b * BLOCK, BLOCK), BLOCK), :]
                + rand[table[first_last + chunk * steps + i * (sub // BLOCK) + b]]
                for b in range(sub // BLOCK)
            ],
            axis=0,
        )

    def reduce_step(base, rand, sums, send, recv, t, waits):
        for h, _, i in parts:
            chunk = lax.rem(z + 1 + t, rows) if h else lax.rem(z + 2 * rows - 1 - t, rows)
            own = own_part(base, rand, chunk, i)
            if waits is True:
                reduce(sums, send, recv, t - 1, h, i).wait_recv()
            elif waits is not False:

                @pl.when(waits)
                def _():
                    reduce(sums, send, recv, t - 1, h, i).wait_recv()

            part = pl.ds(i * sub, sub)
            sums[t, part, :] = (sums[t, part, :].astype(jnp.float32) + own).astype(low)
            reduce(sums, send, recv, t, h, i).start()

    def finish(base, rand, sums, send, recv, fin, land, w):
        copies = []
        for h, _, i in parts:
            own = own_part(base, rand, z, i)
            reduce(sums, send, recv, rows - 2, h, i).wait_recv()
            part = pl.ds(i * sub, sub)
            fin[part, :] = (sums[rows - 1, part, :].astype(jnp.float32) + own).astype(low)
        for d in range(1, cols):
            part = aligned(lax.rem(c + d, cols), tok)
            copies.append(push(fin.at[part, :], land.at[c], back_send.at[w, d], back_recv.at[w, d], across[d]))
        return copies

    dk_ring = (dk_base, dk_rand, k_sum, dk_send, dk_recv)
    dv_ring = (dv_base, dv_rand, v_sum, dv_send, dv_recv)

    def give(i, src, dst, j):
        part = aligned(lax.rem(c + 1 + j, cols), tok)
        to = at(z, c + 1 + j)
        return wire(src.at[part, :], dst.at[:, mine_wide], out_send.at[i, j], out_recv.at[i, j], to)

    outs = ((0, ax, a_out), (1, dqx, dq_out))

    def rest_step(u, _):
        reduce_step(*dv_ring, u, u > 0)
        for w in range(share):
            j = u * share + w
            pair(make_rest, j)

            @pl.when(j < cols - 1)
            def _():
                for out in outs:
                    give(*out, j).start()

        return 0

    lax.fori_loop(0, rows - 1 - early, rest_step, 0)
    for i, src, dst in outs:
        local.append(move(src.at[mine, :], dst.at[:, mine_wide], own_sem.at[4 + i]))
    gp = g1.at[z]
    gp[:heads, :] = gq_acc[...]
    gp[heads:, :] = jnp.broadcast_to(gk_acc[...] / kg_ref[pl.ds(c, 1), :], (heads, head))

    reduce_step(*dk_ring, 0, False)
    one = [push(gp, gp, g1_send.at[d], g1_recv.at[d], along[d]) for d in range(1, rows)]
    reduce_step(*dv_ring, rows - 1 - early, True)

    def both_step(u, _):
        reduce_step(*dk_ring, u, True)
        reduce_step(*dv_ring, u + rows - 1 - early, True)
        return 0

    lax.fori_loop(1, early, both_step, 0)
    for copy in one:
        copy.wait()
    g2[dp] = jnp.sum(g1[...], 0)
    two = [push(g2.at[dp], g2.at[dp], g2_send.at[d], g2_recv.at[d], over[d]) for d in range(1, depth)]
    back = finish(*dv_ring, v_fin, v_land, 1)

    def dk_step(u, _):
        reduce_step(*dk_ring, u, True)
        return 0

    lax.fori_loop(early, rows - 2, dk_step, 0)
    for copy in two:
        copy.wait()
    g3[c] = jnp.sum(g2[...], 0)
    three = [push(g3.at[c], g3.at[c], g3_send.at[d], g3_recv.at[d], across[d]) for d in range(1, cols)]
    reduce_step(*dk_ring, rows - 2, True)
    for copy in back:
        copy.wait()
    v_land[c] = v_fin[mine, :]
    for i in range(cols):
        dv_out[:, cut[i]] = v_land[i]
    back = finish(*dk_ring, k_fin, k_land, 0)

    for copy in three:
        copy.wait()
    gq_out[...] = g3[z, pl.ds(c, 1), :]
    gk_out[...] = jnp.concatenate([g3[i, cols : cols + 1, :] for i in range(cols)], axis=0)
    k_land[c] = k_fin[mine, :]
    for copy in back:
        copy.wait()
    for i in range(cols):
        raw = key_ref[:, cut[i]].astype(jnp.float32)
        scale = lax.rsqrt(jnp.mean(raw * raw, -1, keepdims=True) + EPSILON)
        unit = raw * scale
        gd = kg_ref[i : i + 1, :] * k_land[i].astype(jnp.float32)
        dk_out[:, cut[i]] = (scale * (gd - unit * jnp.mean(unit * gd, -1, keepdims=True))).astype(low)

    for t in range(rows - 1):
        gain_copy(t).wait_send()
        for h, _, i in parts:
            gather(*k_ring, t, h, i).wait_send()
            gather(*v_ring, t, h, i).wait_send()
            reduce(*dk_ring[2:], t, h, i).wait_send()
            reduce(*dv_ring[2:], t, h, i).wait_send()
    for j in range(cols - 1):
        for out in outs:
            give(*out, j).wait()
    for copy in local:
        copy.wait()


def make_table(rows, cols, per, lists):
    _, z, c = place(cols)
    steps = cols * per
    here = lax.dynamic_slice_in_dim(lists, z * steps, steps, 0)[:, WINDOW + GLOBALS :]
    turned = lax.dynamic_slice_in_dim(jnp.concatenate([here, here]), per * (c + 1) % steps, steps, 0).reshape(-1)
    order = jnp.arange(turned.shape[0], dtype=jnp.int32)
    same = (turned[:, None] == turned[None, :]) & (order[None, :] < order[:, None])
    prev = jnp.max(jnp.where(same, order[None, :] + 1, 0), axis=1)
    ids = jnp.arange(lists.shape[0], dtype=jnp.int32)
    last = jnp.max(jnp.where(ids[:, None] == turned[None, :], order[None, :] + 1, 0), axis=1)
    return jnp.concatenate([turned, prev, last]).astype(jnp.int32)


def on_device(depth, queries, keys, values, grad_out, q_gain, k_gain, block_lists):
    cols = k_gain.shape[0]
    rows = lax.axis_size("seq") // cols
    _, tok, wide = queries.shape
    head = q_gain.shape[1]
    width = wide // cols
    heads = width // head
    group = cols * tok
    steps = group // BLOCK
    lists = block_lists[0]
    randoms = lists.shape[1] - WINDOW - GLOBALS
    table = make_table(rows, cols, tok // BLOCK, lists)
    low, full = jnp.bfloat16, jnp.float32
    sem = pltpu.SemaphoreType.DMA
    ring = (rows, 2 * SUBS)
    tile = 2 * heads
    flops = 6 * 2 * group * heads * lists.shape[1] * BLOCK * head
    a, dq, dk, dv, gain_q, gain_k = pl.pallas_call(
        functools.partial(kernel, rows, cols, depth, randoms),
        out_shape=(
            jax.ShapeDtypeStruct((tok, wide), low),
            jax.ShapeDtypeStruct((tok, wide), low),
            jax.ShapeDtypeStruct((tok, head * cols), low),
            jax.ShapeDtypeStruct((tok, head * cols), low),
            jax.ShapeDtypeStruct((1, head), full),
            jax.ShapeDtypeStruct((cols, head), full),
        ),
        in_specs=[pl.BlockSpec(memory_space=pltpu.SMEM)] + [ANY] * 4 + [VMEM] * 3,
        out_specs=(ANY, ANY, VMEM, VMEM, VMEM, VMEM),
        scratch_shapes=[
            pltpu.VMEM((group, width), low),
            pltpu.VMEM((group, width), low),
            pltpu.VMEM((group, head), low),
            pltpu.VMEM((rows * steps, BLOCK, head), low),
            pltpu.VMEM((rows * steps, BLOCK, head), low),
            pltpu.VMEM((8, head), full),
            pltpu.VMEM((cols, 8, head), full),
            pltpu.VMEM((rows, cols, head), full),
            pltpu.VMEM((steps, heads * BLOCK, head), low),
            pltpu.VMEM((steps, heads * BLOCK, lists.shape[1] * BLOCK), low),
            pltpu.VMEM((rows * group, head), full),
            pltpu.VMEM((rows * group, head), full),
            pltpu.VMEM((steps * randoms + 1, BLOCK, head), full),
            pltpu.VMEM((steps * randoms + 1, BLOCK, head), full),
            pltpu.VMEM((heads, head), full),
            pltpu.VMEM((1, head), full),
            pltpu.VMEM((group, width), low),
            pltpu.VMEM((group, width), low),
            pltpu.VMEM((rows, group, head), low),
            pltpu.VMEM((rows, group, head), low),
            pltpu.VMEM((group, head), low),
            pltpu.VMEM((group, head), low),
            pltpu.VMEM((cols, tok, head), low),
            pltpu.VMEM((cols, tok, head), low),
            pltpu.VMEM((rows, tile, head), full),
            pltpu.VMEM((depth, tile, head), full),
            pltpu.VMEM((cols, tile, head), full),
            sem((6,)),
            sem((2, cols)),
            sem((2, cols)),
            sem((2, cols)),
            sem((2, cols)),
            sem((cols,)),
            sem((cols,)),
            sem(ring),
            sem(ring),
            sem(ring),
            sem(ring),
            sem((rows,)),
            sem((rows,)),
            sem((2, cols)),
            sem((2, cols)),
            sem(ring),
            sem(ring),
            sem(ring),
            sem(ring),
            sem((2, cols)),
            sem((2, cols)),
            sem((rows,)),
            sem((rows,)),
            sem((depth,)),
            sem((depth,)),
            sem((cols,)),
            sem((cols,)),
        ],
        compiler_params=pltpu.CompilerParams(
            collective_id=0, has_side_effects=True, vmem_limit_bytes=LIMIT
        ),
        cost_estimate=pl.CostEstimate(flops=flops, bytes_accessed=16 << 20, transcendentals=0),
    )(
        table,
        queries[0],
        grad_out[0],
        keys[0],
        values.reshape(tok // BLOCK, BLOCK, head * cols),
        keys[0],
        q_gain,
        k_gain,
    )
    return a[None], dq[None], dk[None], dv[None], gain_q, gain_k


def solution(mesh):
    spec = P("dp", "seq", None)
    return jax.shard_map(
        functools.partial(on_device, mesh.shape["dp"]),
        mesh=mesh,
        in_specs=(spec, spec, spec, spec, P("seq", None), P(), P("dp", None, None)),
        out_specs=(spec, spec, spec, spec, P("seq", None), P()),
        check_vma=False,
    )
```

```python
import functools
import math

import jax
import jax.numpy as jnp
from jax import lax
from jax.experimental import pallas as pl
from jax.experimental.pallas import tpu as pltpu
from jax.sharding import PartitionSpec as P

EPSILON = 1e-06
BLOCK = 64
SUBS = 2
MESH = pl.DeviceIdType.MESH
ANY = pl.BlockSpec(memory_space=pl.ANY)
VMEM = pl.BlockSpec(memory_space=pltpu.VMEM)
LIMIT = 60 * 1024 * 1024
WINDOW, GLOBALS = 3, 2
LAG, GO_FROM, STRIDE = 2, 3, 3
PIECES = 2


def place(cols):
    seq = lax.axis_index("seq")
    return lax.axis_index("dp"), seq // cols, seq % cols


def greet(devices):
    barrier = pltpu.get_barrier_semaphore()
    for device in devices:
        pl.semaphore_signal(barrier, inc=1, device_id=device, device_id_type=MESH)
    pl.semaphore_wait(barrier, len(devices))


def wire(src, dst, send_sem, recv_sem, device):
    return pltpu.make_async_remote_copy(
        src_ref=src,
        dst_ref=dst,
        send_sem=send_sem,
        recv_sem=recv_sem,
        device_id=device,
        device_id_type=MESH,
    )


def push(*args):
    copy = wire(*args)
    copy.start()
    return copy


def move(src, dst, sem):
    copy = pltpu.make_async_copy(src, dst, sem)
    copy.start()
    return copy


def aligned(index, size):
    return pl.ds(pl.multiple_of(index * size, size), size)


def dot(a, b, dims):
    return lax.dot_general(a, b, (dims, ((), ())), preferred_element_type=jnp.float32)


def kernel(
    rows,
    cols,
    depth,
    randoms,
    table,
    q_ref,
    go_ref,
    k_ref,
    v_ref,
    qg_ref,
    kg_ref,
    a_out,
    dq_out,
    k_land,
    v_land,
    g3,
    qx,
    gox,
    kx,
    kall,
    vall,
    gain,
    gx,
    gz,
    gq_own,
    qn,
    probs,
    dk_base,
    dv_base,
    dk_rand,
    dv_rand,
    gq_acc,
    gk_acc,
    ax,
    dqx,
    k_sum,
    v_sum,
    k_fin,
    v_fin,
    g1,
    g2,
    g2_sum,
    own_sem,
    in_send,
    in_recv,
    kv_send,
    kv_recv,
    gx_send,
    gx_recv,
    k_send,
    k_recv,
    v_send,
    v_recv,
    gz_send,
    gz_recv,
    out_send,
    out_recv,
    dk_send,
    dk_recv,
    dv_send,
    dv_recv,
    back_send,
    back_recv,
    g1_send,
    g1_recv,
    g2_send,
    g2_recv,
    g3_send,
    g3_recv,
):
    dp, z, c = place(cols)
    tok = q_ref.shape[0]
    width = q_ref.shape[1] // cols
    head = k_ref.shape[1] // cols
    heads = width // head
    group = cols * tok
    per = tok // BLOCK
    steps = group // BLOCK
    blocks = rows * steps
    sub = group // (2 * SUBS)
    score_scale = 1.0 / math.sqrt(head)
    low = jnp.bfloat16
    first_prev, first_last = steps * randoms, 2 * steps * randoms

    def at(zz, cc):
        return (dp, lax.rem(zz, rows) * cols + lax.rem(cc, cols))

    across = {d: at(z, c + d) for d in range(1, cols)}
    along = {d: at(z + d, c) for d in range(1, rows)}
    over = {d: (lax.rem(dp + d, depth), z * cols + c) for d in range(1, depth)}
    right, left = along[1], along[rows - 1]
    mine = aligned(c, tok)
    mine_wide = aligned(c, width)
    parts = [(h, s, h * SUBS + s) for s in range(SUBS) for h in range(2)]

    gain[...] = jnp.broadcast_to(qg_ref[...], gain.shape)
    greet(list(across.values()) + list(along.values()) + list(over.values()))

    small, local = [], []
    for d in range(1, cols):
        part = aligned(lax.rem(c + d, cols), head)
        small.append(push(k_ref.at[:, part], kx.at[mine, :], kv_send.at[0, d], kv_recv.at[0, d], across[d]))
        small.append(push(gain, gx.at[c], gx_send.at[d], gx_recv.at[d], across[d]))
    own_blocks = pl.ds(z * steps + c * per, per)
    late = []
    for d in range(1, cols):
        part = aligned(lax.rem(c + d, cols), head)
        late.append(push(v_ref.at[:, :, part], vall.at[own_blocks], kv_send.at[1, d], kv_recv.at[1, d], across[d]))
    own_k = move(k_ref.at[:, aligned(c, head)], kx.at[mine, :], own_sem.at[0])
    own_v = move(v_ref.at[:, :, aligned(c, head)], vall.at[own_blocks], own_sem.at[1])

    def bring(i, src, dst, d):
        part = aligned(lax.rem(c + d, cols), width)
        return push(src.at[:, part], dst.at[mine, :], in_send.at[i, d], in_recv.at[i, d], across[d])

    q_in = [bring(0, q_ref, qx, d) for d in range(1, cols)]
    own_q = move(q_ref.at[:, mine_wide], qx.at[mine, :], own_sem.at[2])
    own_go = move(go_ref.at[:, mine_wide], gox.at[mine, :], own_sem.at[3])
    for ref in (dk_base, dv_base, gq_acc, gk_acc):
        ref[...] = jnp.zeros_like(ref)
    for ref in (dk_rand, dv_rand, k_sum, v_sum):
        ref[0] = jnp.zeros(ref.shape[1:], ref.dtype)

    own_k.wait()
    for copy in small:
        copy.wait()
    raw_key = kx[...].astype(jnp.float32)
    scale = lax.rsqrt(jnp.mean(raw_key * raw_key, -1, keepdims=True) + EPSILON)
    normed_key = (raw_key * scale * kg_ref[pl.ds(c, 1), :]).astype(low)
    kall[pl.ds(z * steps, steps)] = normed_key.reshape(steps, BLOCK, head)
    gx[c] = gain[...]
    gz[...] = jnp.concatenate([gx[i, :1, :] for i in range(cols)], axis=0)
    served = [wire(gz, gq_own, gz_send.at[d], gz_recv.at[0], along[d]) for d in range(1, rows)]

    @pl.when(z == c)
    def _():
        for copy in served:
            copy.start()
        gq_own[...] = gz[...]


    def gather(ref, send, recv, t, h, i):
        slot = lax.rem(z + t, rows) if h else lax.rem(z + rows - t, rows)
        part = pl.ds(slot * steps + i * (sub // BLOCK), sub // BLOCK)
        return wire(ref.at[part], ref.at[part], send.at[t, i], recv.at[t, i], left if h else right)

    def gather_step(ref, send, recv, t, waits=True):
        for h, _, i in parts:
            if waits:
                gather(ref, send, recv, t - 1, h, i).wait_recv()
            gather(ref, send, recv, t, h, i).start()

    k_ring, v_ring = (kall, k_send, k_recv), (vall, v_send, v_recv)

    lag, lag_out, go_from = LAG, rows // 2, GO_FROM
    go_in = []
    for t in range(rows - 1):
        gather_step(*k_ring, t, t > 0)
        if t >= lag:
            if t == lag:
                own_v.wait()
                for copy in late:
                    copy.wait()
            gather_step(*v_ring, t - lag, t > lag)
        if t >= go_from:
            more = -(-(cols - 1) // (rows - 1 - go_from))
            for d in [-STRIDE * (j + 1) % cols for j in range(cols - 1)][(t - go_from) * more : (t - go_from + 1) * more]:
                go_in.append(bring(1, go_ref, gox, d))
    for h, _, i in parts:
        gather(*k_ring, rows - 2, h, i).wait_recv()

    @pl.when(z != c)
    def _():
        served[0].wait_recv()

    own_q.wait()
    for copy in q_in:
        copy.wait()

    cut = [slice(h * head, (h + 1) * head) for h in range(heads)]
    gains = [gq_own[h : h + 1, :] for h in range(heads)]

    def owner(j):
        return lax.rem(c + STRIDE * (j + 1), cols)

    def block_of(i):
        return per * owner(i // per) + i % per

    def fixed(n):
        return [lax.rem(z * steps + n + s + blocks - WINDOW // 2, blocks) for s in range(WINDOW)] + list(range(GLOBALS))

    def listed(ref, n):
        ids = fixed(n) + [table[n * randoms + s] for s in range(randoms)]
        return jnp.concatenate([ref[b] for b in ids], axis=0)

    def unit_queries(n):
        raw = [qx[aligned(n, BLOCK), s].astype(jnp.float32) for s in cut]
        scales = [lax.rsqrt(jnp.mean(x * x, -1, keepdims=True) + EPSILON) for x in raw]
        return [x * s for x, s in zip(raw, scales)], scales

    def cotangents(n):
        return jnp.concatenate([gox[aligned(n, BLOCK), s] for s in cut], axis=0)

    def spread(base, rand, i, n, terms):
        for s, b in enumerate(fixed(n)):
            base[aligned(b, BLOCK), :] += terms[s * BLOCK : (s + 1) * BLOCK]
        for s in range(randoms):
            first = (WINDOW + GLOBALS + s) * BLOCK
            rand[i * randoms + s + 1] = rand[table[first_prev + n * randoms + s]] + terms[first : first + BLOCK]

    def make_probs(i):
        n = block_of(i)
        units, _ = unit_queries(n)
        normed = jnp.concatenate([(u * g).astype(low) for u, g in zip(units, gains)], axis=0)
        qn[n] = normed
        scores = dot(normed, listed(kall, n), ((1,), (1,)))
        expo = jnp.exp2(scores * (score_scale * math.log2(math.e)))
        probs[n] = (expo * (1.0 / jnp.sum(expo, axis=1, keepdims=True))).astype(low)

    def make_dv(i):
        n = block_of(i)
        spread(dv_base, dv_rand, i, n, dot(probs[n], cotangents(n), ((0,), (0,))))

    def make_rest(i):
        n = block_of(i)
        key, value, grad, prob = listed(kall, n), listed(vall, n), cotangents(n), probs[n]
        out = dot(prob, value, ((1,), (0,)))
        dprobs = dot(grad, value, ((1,), (1,)))
        delta = jnp.sum(out * grad.astype(jnp.float32), axis=1, keepdims=True)
        dscores = (prob.astype(jnp.float32) * (dprobs - delta)).astype(low)
        dq = dot(dscores, key, ((1,), (0,))) * score_scale
        dk = dot(dscores, qn[n], ((0,), (0,))) * score_scale
        spread(dk_base, dk_rand, i, n, dk)
        gk_acc[...] += jnp.sum(dk * key.astype(jnp.float32), axis=0, keepdims=True)
        units, scales = unit_queries(n)
        for h in range(heads):
            part = slice(h * BLOCK, (h + 1) * BLOCK)
            ax[aligned(n, BLOCK), cut[h]] = out[part].astype(low)
            d, unit = dq[part], units[h]
            gq_acc[h : h + 1, :] += jnp.sum(d * unit, 0, keepdims=True)
            gd = gains[h] * d
            dqx[aligned(n, BLOCK), cut[h]] = (
                scales[h] * (gd - unit * jnp.mean(unit * gd, -1, keepdims=True))
            ).astype(low)

    def pair(work, j):
        for p in range(per):
            work(j * per + p)

    early = rows - 1 - lag
    share = cols // lag if lag else cols

    def probs_pair(j):
        pair(make_probs, j)
        return 0

    def probs_step(u, _):
        gather_step(*v_ring, u + early)
        lax.fori_loop(0, share, lambda w, _: probs_pair(u * share + w), 0)
        return 0

    if lag:
        lax.fori_loop(0, lag, probs_step, 0)
    else:
        for w in range(cols):
            pair(make_probs, w)


    @pl.when(z == c)
    def _():
        for copy in served:
            copy.wait_send()

    for t in range(rows - 2):
        for h, _, i in parts:
            gather(*k_ring, t, h, i).wait_send()
            gather(*v_ring, t, h, i).wait_send()
    own_go.wait()
    for copy in go_in:
        copy.wait()

    def dv_step(j, _):
        pair(make_dv, j)
        return 0

    lax.fori_loop(0, cols, dv_step, 0)
    for h, _, i in parts:
        gather(*v_ring, rows - 2, h, i).wait_recv()
        gather(*k_ring, rows - 2, h, i).wait_send()
        gather(*v_ring, rows - 2, h, i).wait_send()

    def reduce(sums, send, recv, t, h, i):
        part = pl.ds(i * sub, sub)
        return wire(sums.at[t, part, :], sums.at[t + 1, part, :], send.at[t, i], recv.at[t, i], left if h else right)

    def own_part(base, rand, chunk, i):
        start = chunk * group + i * sub
        return jnp.concatenate(
            [
                base[pl.ds(pl.multiple_of(start + b * BLOCK, BLOCK), BLOCK), :]
                + rand[table[first_last + chunk * steps + i * (sub // BLOCK) + b]]
                for b in range(sub // BLOCK)
            ],
            axis=0,
        )

    def reduce_step(base, rand, sums, send, recv, t, waits):
        for h, _, i in parts:
            chunk = lax.rem(z + 1 + t, rows) if h else lax.rem(z + 2 * rows - 1 - t, rows)
            own = own_part(base, rand, chunk, i)
            if waits is True:
                reduce(sums, send, recv, t - 1, h, i).wait_recv()
            elif waits is not False:

                @pl.when(waits)
                def _():
                    reduce(sums, send, recv, t - 1, h, i).wait_recv()

            part = pl.ds(i * sub, sub)
            sums[t, part, :] = (sums[t, part, :].astype(jnp.float32) + own).astype(low)
            reduce(sums, send, recv, t, h, i).start()

    def finish(base, rand, sums, send, recv, fin, land, w):
        for h, _, i in parts:
            own = own_part(base, rand, z, i)
            reduce(sums, send, recv, rows - 2, h, i).wait_recv()
            part = pl.ds(i * sub, sub)
            fin[part, :] = (sums[rows - 1, part, :].astype(jnp.float32) + own).astype(low)
            for cc in range(i * sub // tok, (i + 1) * sub // tok):
                d = lax.rem(cc - c + cols, cols)

                @pl.when(d > 0)
                def _():
                    back(fin, land, w, cc, d).start()

        local.append(move(fin.at[mine, :], land.at[c], own_sem.at[6 + w]))

    def back(fin, land, w, cc, d):
        return wire(fin.at[pl.ds(cc * tok, tok), :], land.at[c], back_send.at[w, d], back_recv.at[w, d], at(z, cc))

    def finish_wait(fin, land, w):
        for d in range(1, cols):
            back(fin, land, w, 0, d).wait()

    dk_ring = (dk_base, dk_rand, k_sum, dk_send, dk_recv)
    dv_ring = (dv_base, dv_rand, v_sum, dv_send, dv_recv)

    def give(i, src, dst, j):
        part = aligned(owner(j), tok)
        to = at(z, owner(j))
        return wire(src.at[part, :], dst.at[:, mine_wide], out_send.at[i, j], out_recv.at[i, j], to)

    outs = ((0, ax, a_out), (1, dqx, dq_out))

    early = rows - 1 - lag_out
    share = cols // lag_out

    def rest_step(u, _):
        reduce_step(*dv_ring, u, u > 0)
        for w in range(share):
            j = u * share + w
            pair(make_rest, j)

            @pl.when(j < cols - 1)
            def _():
                for out in outs:
                    give(*out, j).start()

        return 0

    lax.fori_loop(0, lag_out, rest_step, 0)
    for i, src, dst in outs:
        local.append(move(src.at[mine, :], dst.at[:, mine_wide], own_sem.at[4 + i]))
    gp = g1.at[z]
    gp[:heads, :] = gq_acc[...]
    gp[heads:, :] = jnp.broadcast_to(gk_acc[...] / kg_ref[pl.ds(c, 1), :], (heads, head))

    reduce_step(*dk_ring, 0, False)
    one = [push(gp, gp, g1_send.at[d], g1_recv.at[d], along[d]) for d in range(1, rows)]
    reduce_step(*dv_ring, lag_out, True)

    def both_step(u, _):
        reduce_step(*dk_ring, u, True)
        reduce_step(*dv_ring, u + lag_out, True)
        return 0

    lax.fori_loop(1, early, both_step, 0)
    for copy in one:
        copy.wait()
    g2[dp] = jnp.sum(g1[...], 0)
    two = [push(g2.at[dp], g2.at[dp], g2_send.at[d], g2_recv.at[d], over[d]) for d in range(1, depth)]
    finish(*dv_ring, v_fin, v_land, 1)

    def dk_step(u, _):
        reduce_step(*dk_ring, u, True)
        return 0

    lax.fori_loop(early, rows - 2, dk_step, 0)
    for copy in two:
        copy.wait()
    g2_sum[...] = jnp.sum(g2[...], 0)
    three = [push(g2_sum, g3.at[c], g3_send.at[d], g3_recv.at[d], across[d]) for d in range(1, cols)]
    local.append(move(g2_sum, g3.at[c], own_sem.at[8]))
    reduce_step(*dk_ring, rows - 2, True)
    finish_wait(v_fin, v_land, 1)
    for t in range(rows - 2):
        for h, _, i in parts:
            reduce(*dv_ring[2:], t, h, i).wait_send()
            reduce(*dk_ring[2:], t, h, i).wait_send()
    finish(*dk_ring, k_fin, k_land, 0)

    for j in range(cols - 1):
        for out in outs:
            give(*out, j).wait()
    for copy in three:
        copy.wait()
    for h, _, i in parts:
        reduce(*dv_ring[2:], rows - 2, h, i).wait_send()
        reduce(*dk_ring[2:], rows - 2, h, i).wait_send()
    for copy in local:
        copy.wait()
    finish_wait(k_fin, k_land, 0)


def final_kernel(
    cols, a_ref, dq_ref, dk_ref, dv_ref, g_ref, k_ref, kg_ref, a_out, dq_out, dk_out, dv_out, gq_out, gk_out,
    a_buf, dq_buf, dk_in, dv_in, g_in, key, kg, dk_buf, dv_buf, gq_buf, gk_buf, sem,
):
    _, z, c = place(cols)
    tok, head = dk_in.shape[1:]
    ins = [move(src, dst, sem.at[i, 0, 0]) for i, (src, dst) in enumerate(((k_ref, key), (dk_ref, dk_in), (kg_ref, kg), (dv_ref, dv_in), (g_ref, g_in)))]
    piece = tok // PIECES
    cuts = [pl.ds(p * piece, piece) for p in range(PIECES)]
    wide = ((a_ref, a_buf, a_out), (dq_ref, dq_buf, dq_out))
    come = [move(src.at[p, :], buf.at[p, :], sem.at[9, i, n]) for i, (src, buf, _) in enumerate(wide) for n, p in enumerate(cuts)]
    big = []
    for i, (_, buf, dst) in enumerate(wide):
        for n, p in enumerate(cuts):
            come[i * PIECES + n].wait()
            big.append(move(buf.at[p, :], dst.at[p, :], sem.at[10, i, n]))
    for copy in ins:
        copy.wait()
    cut = [slice(i * head, (i + 1) * head) for i in range(cols)]
    for i in range(cols):
        raw = key[:, cut[i]].astype(jnp.float32)
        scale = lax.rsqrt(jnp.mean(raw * raw, -1, keepdims=True) + EPSILON)
        unit = raw * scale
        gd = kg[i : i + 1, :] * dk_in[i].astype(jnp.float32)
        dk_buf[:, cut[i]] = (scale * (gd - unit * jnp.mean(unit * gd, -1, keepdims=True))).astype(jnp.bfloat16)
        dv_buf[:, cut[i]] = dv_in[i]
    gq_buf[...] = g_in[z, pl.ds(c, 1), :]
    gk_buf[...] = jnp.concatenate([g_in[i, cols : cols + 1, :] for i in range(cols)], axis=0)
    for i, (src, dst) in enumerate(((dk_buf, dk_out), (dv_buf, dv_out), (gq_buf, gq_out), (gk_buf, gk_out))):
        big.append(move(src, dst, sem.at[5 + i, 0, 0]))
    for copy in big:
        copy.wait()


def finalize(cols, a, dq, dk, dv, g, keys, k_gain):
    tok, wide = keys.shape
    head = wide // cols
    low, full = jnp.bfloat16, jnp.float32
    outs = (
        jax.ShapeDtypeStruct(a.shape, low),
        jax.ShapeDtypeStruct(dq.shape, low),
        jax.ShapeDtypeStruct((tok, wide), low),
        jax.ShapeDtypeStruct((tok, wide), low),
        jax.ShapeDtypeStruct((1, head), full),
        jax.ShapeDtypeStruct((cols, head), full),
    )
    return pl.pallas_call(
        functools.partial(final_kernel, cols),
        out_shape=outs,
        in_specs=[ANY] * 7,
        out_specs=(ANY,) * 6,
        scratch_shapes=[pltpu.VMEM(x.shape, x.dtype) for x in (a, dq, dk, dv, g, keys, k_gain) + outs[2:]]
        + [pltpu.SemaphoreType.DMA((11, 2, PIECES))],
        compiler_params=pltpu.CompilerParams(vmem_limit_bytes=LIMIT),
        cost_estimate=pl.CostEstimate(flops=0, bytes_accessed=8 << 20, transcendentals=0),
    )(a, dq, dk, dv, g, keys, k_gain)


def make_table(rows, cols, per, lists):
    _, z, c = place(cols)
    steps = cols * per
    here = lax.dynamic_slice_in_dim(lists, z * steps, steps, 0)[:, WINDOW + GLOBALS :]
    randoms = here.shape[1]
    here = here.reshape(-1)
    place_of = jnp.arange(here.shape[0], dtype=jnp.int32)
    block, slot = place_of // randoms, place_of % randoms
    turn = (STRIDE * (block // per - c + cols) - 1) % cols
    order = (turn * per + block % per) * randoms + slot + 1
    same = (here[:, None] == here[None, :]) & (order[None, :] < order[:, None])
    prev = jnp.max(jnp.where(same, order[None, :], 0), axis=1)
    ids = jnp.arange(lists.shape[0], dtype=jnp.int32)
    last = jnp.max(jnp.where(ids[:, None] == here[None, :], order[None, :], 0), axis=1)
    return jnp.concatenate([here, prev, last]).astype(jnp.int32)


def on_device(depth, queries, keys, values, grad_out, q_gain, k_gain, block_lists):
    cols = k_gain.shape[0]
    rows = lax.axis_size("seq") // cols
    _, tok, wide = queries.shape
    head = q_gain.shape[1]
    width = wide // cols
    heads = width // head
    group = cols * tok
    steps = group // BLOCK
    lists = block_lists[0]
    randoms = lists.shape[1] - WINDOW - GLOBALS
    table = make_table(rows, cols, tok // BLOCK, lists)
    low, full = jnp.bfloat16, jnp.float32
    sem = pltpu.SemaphoreType.DMA
    ring = (rows, 2 * SUBS)
    tile = 2 * heads
    flops = 6 * 2 * group * heads * lists.shape[1] * BLOCK * head
    a, dq, dk, dv, g = pl.pallas_call(
        functools.partial(kernel, rows, cols, depth, randoms),
        out_shape=(
            jax.ShapeDtypeStruct((tok, wide), low),
            jax.ShapeDtypeStruct((tok, wide), low),
            jax.ShapeDtypeStruct((cols, tok, head), low),
            jax.ShapeDtypeStruct((cols, tok, head), low),
            jax.ShapeDtypeStruct((cols, tile, head), full),
        ),
        in_specs=[pl.BlockSpec(memory_space=pltpu.SMEM)] + [ANY] * 4 + [VMEM] * 2,
        out_specs=(ANY,) * 5,
        scratch_shapes=[
            pltpu.VMEM((group, width), low),
            pltpu.VMEM((group, width), low),
            pltpu.VMEM((group, head), low),
            pltpu.VMEM((rows * steps, BLOCK, head), low),
            pltpu.VMEM((rows * steps, BLOCK, head), low),
            pltpu.VMEM((8, head), full),
            pltpu.VMEM((cols, 8, head), full),
            pltpu.VMEM((cols, head), full),
            pltpu.VMEM((cols, head), full),
            pltpu.VMEM((steps, heads * BLOCK, head), low),
            pltpu.VMEM((steps, heads * BLOCK, lists.shape[1] * BLOCK), low),
            pltpu.VMEM((rows * group, head), full),
            pltpu.VMEM((rows * group, head), full),
            pltpu.VMEM((steps * randoms + 1, BLOCK, head), full),
            pltpu.VMEM((steps * randoms + 1, BLOCK, head), full),
            pltpu.VMEM((heads, head), full),
            pltpu.VMEM((1, head), full),
            pltpu.VMEM((group, width), low),
            pltpu.VMEM((group, width), low),
            pltpu.VMEM((rows, group, head), low),
            pltpu.VMEM((rows, group, head), low),
            pltpu.VMEM((group, head), low),
            pltpu.VMEM((group, head), low),
            pltpu.VMEM((rows, tile, head), full),
            pltpu.VMEM((depth, tile, head), full),
            pltpu.VMEM((tile, head), full),
            sem((9,)),
            sem((2, cols)),
            sem((2, cols)),
            sem((2, cols)),
            sem((2, cols)),
            sem((cols,)),
            sem((cols,)),
            sem(ring),
            sem(ring),
            sem(ring),
            sem(ring),
            sem((rows,)),
            sem((rows,)),
            sem((2, cols)),
            sem((2, cols)),
            sem(ring),
            sem(ring),
            sem(ring),
            sem(ring),
            sem((2, cols)),
            sem((2, cols)),
            sem((rows,)),
            sem((rows,)),
            sem((depth,)),
            sem((depth,)),
            sem((cols,)),
            sem((cols,)),
        ],
        compiler_params=pltpu.CompilerParams(
            collective_id=0, has_side_effects=True, vmem_limit_bytes=LIMIT
        ),
        cost_estimate=pl.CostEstimate(flops=flops, bytes_accessed=16 << 20, transcendentals=0),
    )(
        table,
        queries[0],
        grad_out[0],
        keys[0],
        values.reshape(tok // BLOCK, BLOCK, head * cols),
        q_gain,
        k_gain,
    )
    a, dq, dk, dv, gain_q, gain_k = finalize(cols, a, dq, dk, dv, g, keys[0], k_gain)
    return a[None], dq[None], dk[None], dv[None], gain_q, gain_k


def solution(mesh):
    spec = P("dp", "seq", None)
    return jax.shard_map(
        functools.partial(on_device, mesh.shape["dp"]),
        mesh=mesh,
        in_specs=(spec, spec, spec, spec, P("seq", None), P(), P("dp", None, None)),
        out_specs=(spec, spec, spec, spec, P("seq", None), P()),
        check_vma=False,
    )
```

```python
import functools
import math

import jax
import jax.numpy as jnp
from jax import lax
from jax.experimental import pallas as pl
from jax.experimental.pallas import tpu as pltpu
from jax.sharding import PartitionSpec as P

EPSILON = 1e-06
BLOCK = 64
SUBS = 1
MESH = pl.DeviceIdType.MESH
ANY = pl.BlockSpec(memory_space=pl.ANY)
VMEM = pl.BlockSpec(memory_space=pltpu.VMEM)
LIMIT = 60 * 1024 * 1024
WINDOW, GLOBALS = 3, 2
GO_AT, STRIDE = (0, 3, 7, 7, 7), 5
PIECES = 2


def place(cols):
    seq = lax.axis_index("seq")
    return lax.axis_index("dp"), seq // cols, seq % cols


def greet(devices):
    barrier = pltpu.get_barrier_semaphore()
    for device in devices:
        pl.semaphore_signal(barrier, inc=1, device_id=device, device_id_type=MESH)
    pl.semaphore_wait(barrier, len(devices))


def wire(src, dst, send_sem, recv_sem, device):
    return pltpu.make_async_remote_copy(
        src_ref=src,
        dst_ref=dst,
        send_sem=send_sem,
        recv_sem=recv_sem,
        device_id=device,
        device_id_type=MESH,
    )


def push(*args):
    copy = wire(*args)
    copy.start()
    return copy


def move(src, dst, sem):
    copy = pltpu.make_async_copy(src, dst, sem)
    copy.start()
    return copy


def aligned(index, size):
    return pl.ds(pl.multiple_of(index * size, size), size)


def dot(a, b, dims):
    return lax.dot_general(a, b, (dims, ((), ())), preferred_element_type=jnp.float32)


def kernel(
    rows,
    cols,
    depth,
    randoms,
    table,
    q_ref,
    go_ref,
    k_ref,
    v_ref,
    qg_ref,
    kg_ref,
    a_out,
    dq_out,
    k_land,
    v_land,
    g3,
    qx,
    gox,
    kx,
    kall,
    vall,
    gain,
    gx,
    gz,
    gq_own,
    qn,
    probs,
    dk_base,
    dv_base,
    dk_rand,
    dv_rand,
    gq_acc,
    gk_acc,
    delta,
    ax,
    dqx,
    k_sum,
    v_sum,
    k_fin,
    v_fin,
    g1,
    g2,
    g2_sum,
    own_sem,
    in_send,
    in_recv,
    kv_send,
    kv_recv,
    gx_send,
    gx_recv,
    k_send,
    k_recv,
    v_send,
    v_recv,
    gz_send,
    gz_recv,
    out_send,
    out_recv,
    dk_send,
    dk_recv,
    dv_send,
    dv_recv,
    back_send,
    back_recv,
    g1_send,
    g1_recv,
    g2_send,
    g2_recv,
    g3_send,
    g3_recv,
):
    dp, z, c = place(cols)
    tok = q_ref.shape[0]
    width = q_ref.shape[1] // cols
    head = k_ref.shape[1] // cols
    heads = width // head
    group = cols * tok
    per = tok // BLOCK
    steps = group // BLOCK
    blocks = rows * steps
    sub = group // (2 * SUBS)
    score_scale = 1.0 / math.sqrt(head)
    low = jnp.bfloat16
    first_prev, first_last = steps * randoms, 2 * steps * randoms

    def at(zz, cc):
        return (dp, lax.rem(zz, rows) * cols + lax.rem(cc, cols))

    across = {d: at(z, c + d) for d in range(1, cols)}
    along = {d: at(z + d, c) for d in range(1, rows)}
    over = {d: (lax.rem(dp + d, depth), z * cols + c) for d in range(1, depth)}
    right, left = along[1], along[rows - 1]
    mine = aligned(c, tok)
    mine_wide = aligned(c, width)
    hops = rows // 2
    parts = [(dr, h, h * SUBS + s) for s in range(SUBS) for h in range(2) for dr in range(2)]

    gain[...] = jnp.broadcast_to(qg_ref[...], gain.shape)
    greet(list(across.values()) + list(along.values()) + list(over.values()))

    small, local = [], []
    for d in range(1, cols):
        part = aligned(lax.rem(c + d, cols), head)
        small.append(push(k_ref.at[:, part], kx.at[mine, :], kv_send.at[0, d], kv_recv.at[0, d], across[d]))
        small.append(push(gain, gx.at[c], gx_send.at[d], gx_recv.at[d], across[d]))
    own_blocks = pl.ds(z * steps + c * per, per)
    late = []
    for d in range(1, cols):
        part = aligned(lax.rem(c + d, cols), head)
        late.append(push(v_ref.at[:, :, part], vall.at[own_blocks], kv_send.at[1, d], kv_recv.at[1, d], across[d]))
    own_k = move(k_ref.at[:, aligned(c, head)], kx.at[mine, :], own_sem.at[0])
    own_v = move(v_ref.at[:, :, aligned(c, head)], vall.at[own_blocks], own_sem.at[1])

    def bring(i, src, dst, d):
        part = aligned(lax.rem(c + d, cols), width)
        return wire(src.at[:, part], dst.at[mine, :], in_send.at[i, d], in_recv.at[i, d], at(z, c + d))

    q_in = [bring(0, q_ref, qx, d) for d in range(1, cols)]
    for copy in q_in:
        copy.start()
    own_q = move(q_ref.at[:, mine_wide], qx.at[mine, :], own_sem.at[2])
    own_go = move(go_ref.at[:, mine_wide], gox.at[mine, :], own_sem.at[3])
    for ref in (dk_base, dv_base, gq_acc, gk_acc):
        ref[...] = jnp.zeros_like(ref)
    for ref in (dk_rand, dv_rand):
        ref[0] = jnp.zeros(ref.shape[1:], ref.dtype)

    own_k.wait()
    for copy in small:
        copy.wait()
    raw_key = kx[...].astype(jnp.float32)
    scale = lax.rsqrt(jnp.mean(raw_key * raw_key, -1, keepdims=True) + EPSILON)
    normed_key = (raw_key * scale * kg_ref[pl.ds(c, 1), :]).astype(low)
    kall[pl.ds(z * steps, steps)] = normed_key.reshape(steps, BLOCK, head)
    gx[c] = gain[...]
    gz[...] = jnp.concatenate([gx[i, :1, :] for i in range(cols)], axis=0)
    served = [wire(gz, gq_own, gz_send.at[d], gz_recv.at[0], along[d]) for d in range(1, rows)]

    @pl.when(z == c)
    def _():
        for copy in served:
            copy.start()
        gq_own[...] = gz[...]


    def gather(ref, send, recv, t, dr, i):
        slot = lax.rem(z + t, rows) if dr else lax.rem(z + rows - t, rows)
        part = pl.ds(slot * steps + i * (sub // BLOCK), sub // BLOCK)
        m = dr * 2 * SUBS + i
        return wire(ref.at[part], ref.at[part], send.at[t, m], recv.at[t, m], left if dr else right)

    def gather_parts(t):
        return [(dr, i) for dr, h, i in parts if t < hops - 1 or h == dr]

    def gather_step(ref, send, recv, t):
        for dr, i in gather_parts(t):
            if t:
                gather(ref, send, recv, t - 1, dr, i).wait_recv()
            gather(ref, send, recv, t, dr, i).start()

    def gather_end(ref, send, recv):
        last = gather_parts(hops - 1)
        for dr, i in gather_parts(hops - 2):
            if (dr, i) not in last:
                gather(ref, send, recv, hops - 2, dr, i).wait_recv()
        for dr, i in last:
            gather(ref, send, recv, hops - 1, dr, i).wait_recv()

    k_ring, v_ring = (kall, k_send, k_recv), (vall, v_send, v_recv)
    order = [-STRIDE * (j + 1) % cols for j in range(cols - 1)]
    go_in = [bring(1, go_ref, gox, d) for d in order]
    for t in range(hops):
        gather_step(*k_ring, t)
        if t == 1:
            own_v.wait()
            for copy in late:
                copy.wait()
        if t:
            gather_step(*v_ring, t - 1)
        for copy in go_in[GO_AT[t] : GO_AT[t + 1]]:
            copy.start()
    gather_end(*k_ring)

    @pl.when(z != c)
    def _():
        served[0].wait_recv()

    own_q.wait()
    for copy in q_in:
        copy.wait()

    cut = [slice(h * head, (h + 1) * head) for h in range(heads)]
    gains = [gq_own[h : h + 1, :] for h in range(heads)]

    def owner(j):
        return lax.rem(c + STRIDE * (j + 1), cols)

    def block_of(i):
        return per * owner(i // per) + i % per

    def fixed(n):
        return [lax.rem(z * steps + n + s + blocks - WINDOW // 2, blocks) for s in range(WINDOW)] + list(range(GLOBALS))

    def listed(ref, n):
        ids = fixed(n) + [table[n * randoms + s] for s in range(randoms)]
        return jnp.concatenate([ref[b] for b in ids], axis=0)

    def unit_queries(n):
        raw = [qx[aligned(n, BLOCK), s].astype(jnp.float32) for s in cut]
        scales = [lax.rsqrt(jnp.mean(x * x, -1, keepdims=True) + EPSILON) for x in raw]
        return [x * s for x, s in zip(raw, scales)], scales

    def cotangents(n):
        return jnp.concatenate([gox[aligned(n, BLOCK), s] for s in cut], axis=0)

    def spread(base, rand, i, n, terms):
        for s, b in enumerate(fixed(n)):
            base[aligned(b, BLOCK), :] += terms[s * BLOCK : (s + 1) * BLOCK]
        for s in range(randoms):
            first = (WINDOW + GLOBALS + s) * BLOCK
            rand[i * randoms + s + 1] = rand[table[first_prev + n * randoms + s]] + terms[first : first + BLOCK]

    def make_probs(i):
        n = block_of(i)
        units, _ = unit_queries(n)
        normed = jnp.concatenate([(u * g).astype(low) for u, g in zip(units, gains)], axis=0)
        qn[n] = normed
        scores = dot(normed, listed(kall, n), ((1,), (1,)))
        expo = jnp.exp2(scores * (score_scale * math.log2(math.e)))
        probs[n] = (expo * (1.0 / jnp.sum(expo, axis=1, keepdims=True))).astype(low)

    def make_out(i):
        n = block_of(i)
        prob, grad = probs[n], cotangents(n)
        out = dot(prob, listed(vall, n), ((1,), (0,)))
        delta[n] = jnp.sum(out * grad.astype(jnp.float32), axis=1, keepdims=True)
        for h in range(heads):
            ax[aligned(n, BLOCK), cut[h]] = out[h * BLOCK : (h + 1) * BLOCK].astype(low)
        spread(dv_base, dv_rand, i, n, dot(prob, grad, ((0,), (0,))))

    def make_dk(i):
        n = block_of(i)
        key = listed(kall, n)
        dprobs = dot(cotangents(n), listed(vall, n), ((1,), (1,)))
        dscores = (probs[n].astype(jnp.float32) * (dprobs - delta[n])).astype(low)
        dk = dot(dscores, qn[n], ((0,), (0,))) * score_scale
        spread(dk_base, dk_rand, i, n, dk)
        gk_acc[...] += jnp.sum(dk * key.astype(jnp.float32), axis=0, keepdims=True)
        probs[n] = dscores

    def make_dq(i):
        n = block_of(i)
        dq = dot(probs[n], listed(kall, n), ((1,), (0,))) * score_scale
        units, scales = unit_queries(n)
        for h in range(heads):
            d, unit = dq[h * BLOCK : (h + 1) * BLOCK], units[h]
            gq_acc[h : h + 1, :] += jnp.sum(d * unit, 0, keepdims=True)
            gd = gains[h] * d
            dqx[aligned(n, BLOCK), cut[h]] = (
                scales[h] * (gd - unit * jnp.mean(unit * gd, -1, keepdims=True))
            ).astype(low)

    def pair(make, j):
        for p in range(per):
            make(j * per + p)

    def probs_step(j, _):
        pair(make_probs, j)
        return 0

    lax.fori_loop(0, cols // 2, probs_step, 0)
    gather_step(*v_ring, hops - 1)
    lax.fori_loop(cols // 2, cols, probs_step, 0)

    @pl.when(z == c)
    def _():
        for copy in served:
            copy.wait_send()

    for t in range(hops):
        for dr, i in gather_parts(t):
            gather(*k_ring, t, dr, i).wait_send()
    own_go.wait()

    gather_end(*v_ring)

    def give(i, src, dst, j):
        part = aligned(owner(j), tok)
        to = at(z, owner(j))
        return wire(src.at[part, :], dst.at[:, mine_wide], out_send.at[i, j], out_recv.at[i, j], to)

    outs = ((0, ax, a_out), (1, dqx, dq_out))

    def out_step(j, _):
        @pl.when(j < cols - 1)
        def _():
            bring(1, go_ref, gox, lax.rem((cols - STRIDE) * (j + 1), cols)).wait_recv()

        pair(make_out, j)

        @pl.when(j < cols - 1)
        def _():
            give(*outs[0], j).start()

        return 0

    lax.fori_loop(0, cols, out_step, 0)

    def reduce(sums, send, recv, t, dr, i):
        part = pl.ds(i * sub, sub)
        m = dr * 2 * SUBS + i
        return wire(
            sums.at[dr, t, part, :], sums.at[dr, t + 1, part, :], send.at[t, m], recv.at[t, m], left if dr else right
        )

    def reduce_parts(t):
        return [(dr, i) for dr, h, i in parts if t or h == dr]

    def own_part(base, rand, chunk, i):
        start = chunk * group + i * sub
        return jnp.concatenate(
            [
                base[pl.ds(pl.multiple_of(start + b * BLOCK, BLOCK), BLOCK), :]
                + rand[table[first_last + chunk * steps + i * (sub // BLOCK) + b]]
                for b in range(sub // BLOCK)
            ],
            axis=0,
        )

    def reduce_step(base, rand, sums, send, recv, t):
        for dr, i in reduce_parts(t):
            far = hops - t
            chunk = lax.rem(z + rows - far, rows) if dr else lax.rem(z + far, rows)
            total = own_part(base, rand, chunk, i)
            part = pl.ds(i * sub, sub)
            if t and (dr, i) in reduce_parts(t - 1):
                reduce(sums, send, recv, t - 1, dr, i).wait_recv()
                total += sums[dr, t, part, :].astype(jnp.float32)
            sums[dr, t, part, :] = total.astype(low)
            reduce(sums, send, recv, t, dr, i).start()

    def reduce_sent(sums, send, recv, t):
        for dr, i in reduce_parts(t):
            reduce(sums, send, recv, t, dr, i).wait_send()

    def finish(base, rand, sums, send, recv, fin, land, w):
        for i in [i for dr, _, i in parts if dr]:
            part = pl.ds(i * sub, sub)
            total = own_part(base, rand, z, i)
            for dr in range(2):
                reduce(sums, send, recv, hops - 1, dr, i).wait_recv()
                total += sums[dr, hops, part, :].astype(jnp.float32)
            fin[part, :] = total.astype(low)
            for cc in range(i * sub // tok, (i + 1) * sub // tok):
                d = lax.rem(cc - c + cols, cols)

                @pl.when(d > 0)
                def _():
                    back(fin, land, w, cc, d).start()

        local.append(move(fin.at[mine, :], land.at[c], own_sem.at[6 + w]))

    def back(fin, land, w, cc, d):
        return wire(fin.at[pl.ds(cc * tok, tok), :], land.at[c], back_send.at[w, d], back_recv.at[w, d], at(z, cc))

    def finish_wait(fin, land, w):
        for d in range(1, cols):
            back(fin, land, w, 0, d).wait()

    dk_ring = (dk_base, dk_rand, k_sum, dk_send, dk_recv)
    dv_ring = (dv_base, dv_rand, v_sum, dv_send, dv_recv)

    def dk_work(start, stop):
        def step(j, _):
            pair(make_dk, j)
            return 0

        lax.fori_loop(start, stop, step, 0)

    def dq_work(start, stop):
        def step(j, _):
            pair(make_dq, j)

            @pl.when(j < cols - 1)
            def _():
                give(*outs[1], j).start()

            return 0

        lax.fori_loop(start, stop, step, 0)

    half = cols // 2
    reduce_step(*dv_ring, 0)
    dk_work(0, half)
    reduce_step(*dv_ring, 1)
    dk_work(half, cols)
    reduce_step(*dk_ring, 0)
    for t in range(hops):
        for dr, i in gather_parts(t):
            gather(*v_ring, t, dr, i).wait_send()
    reduce_step(*dv_ring, 2)
    dq_work(0, half)
    reduce_step(*dk_ring, 1)
    reduce_step(*dv_ring, 3)
    dq_work(half, cols)
    for i, src, dst in outs:
        local.append(move(src.at[mine, :], dst.at[:, mine_wide], own_sem.at[4 + i]))
    gp = g1.at[z]
    gp[:heads, :] = gq_acc[...]
    gp[heads:, :] = jnp.broadcast_to(gk_acc[...] / kg_ref[pl.ds(c, 1), :], (heads, head))
    one = [push(gp, gp, g1_send.at[d], g1_recv.at[d], along[d]) for d in range(1, rows)]
    reduce_step(*dk_ring, 2)
    for copy in one:
        copy.wait()
    g2[dp] = jnp.sum(g1[...], 0)
    two = [push(g2.at[dp], g2.at[dp], g2_send.at[d], g2_recv.at[d], over[d]) for d in range(1, depth)]
    finish(*dv_ring, v_fin, v_land, 1)
    for t in range(hops):
        reduce_sent(*dv_ring[2:], t)
    for copy in go_in:
        copy.wait_send()
    reduce_step(*dk_ring, 3)
    for copy in two:
        copy.wait()
    g2_sum[...] = jnp.sum(g2[...], 0)
    three = [push(g2_sum, g3.at[c], g3_send.at[d], g3_recv.at[d], across[d]) for d in range(1, cols)]
    local.append(move(g2_sum, g3.at[c], own_sem.at[8]))
    finish_wait(v_fin, v_land, 1)
    for t in range(hops - 1):
        reduce_sent(*dk_ring[2:], t)
    finish(*dk_ring, k_fin, k_land, 0)

    for j in range(cols - 1):
        for out in outs:
            give(*out, j).wait()
    for copy in three:
        copy.wait()
    reduce_sent(*dk_ring[2:], hops - 1)
    for copy in local:
        copy.wait()
    finish_wait(k_fin, k_land, 0)


def final_kernel(
    cols, a_ref, dq_ref, dk_ref, dv_ref, g_ref, k_ref, kg_ref, a_out, dq_out, dk_out, dv_out, gq_out, gk_out,
    a_buf, dq_buf, dk_in, dv_in, g_in, key, kg, dk_buf, dv_buf, gq_buf, gk_buf, sem,
):
    _, z, c = place(cols)
    tok, head = dk_in.shape[1:]
    ins = [move(src, dst, sem.at[i, 0, 0]) for i, (src, dst) in enumerate(((k_ref, key), (dk_ref, dk_in), (kg_ref, kg), (dv_ref, dv_in), (g_ref, g_in)))]
    piece = tok // PIECES
    cuts = [pl.ds(p * piece, piece) for p in range(PIECES)]
    wide = ((a_ref, a_buf, a_out), (dq_ref, dq_buf, dq_out))
    come = [move(src.at[p, :], buf.at[p, :], sem.at[9, i, n]) for i, (src, buf, _) in enumerate(wide) for n, p in enumerate(cuts)]
    big = []
    for i, (_, buf, dst) in enumerate(wide):
        for n, p in enumerate(cuts):
            come[i * PIECES + n].wait()
            big.append(move(buf.at[p, :], dst.at[p, :], sem.at[10, i, n]))
    for copy in ins:
        copy.wait()
    cut = [slice(i * head, (i + 1) * head) for i in range(cols)]
    for i in range(cols):
        raw = key[:, cut[i]].astype(jnp.float32)
        scale = lax.rsqrt(jnp.mean(raw * raw, -1, keepdims=True) + EPSILON)
        unit = raw * scale
        gd = kg[i : i + 1, :] * dk_in[i].astype(jnp.float32)
        dk_buf[:, cut[i]] = (scale * (gd - unit * jnp.mean(unit * gd, -1, keepdims=True))).astype(jnp.bfloat16)
        dv_buf[:, cut[i]] = dv_in[i]
    gq_buf[...] = g_in[z, pl.ds(c, 1), :]
    gk_buf[...] = jnp.concatenate([g_in[i, cols : cols + 1, :] for i in range(cols)], axis=0)
    for i, (src, dst) in enumerate(((dk_buf, dk_out), (dv_buf, dv_out), (gq_buf, gq_out), (gk_buf, gk_out))):
        big.append(move(src, dst, sem.at[5 + i, 0, 0]))
    for copy in big:
        copy.wait()


def finalize(cols, a, dq, dk, dv, g, keys, k_gain):
    tok, wide = keys.shape
    head = wide // cols
    low, full = jnp.bfloat16, jnp.float32
    outs = (
        jax.ShapeDtypeStruct(a.shape, low),
        jax.ShapeDtypeStruct(dq.shape, low),
        jax.ShapeDtypeStruct((tok, wide), low),
        jax.ShapeDtypeStruct((tok, wide), low),
        jax.ShapeDtypeStruct((1, head), full),
        jax.ShapeDtypeStruct((cols, head), full),
    )
    return pl.pallas_call(
        functools.partial(final_kernel, cols),
        out_shape=outs,
        in_specs=[ANY] * 7,
        out_specs=(ANY,) * 6,
        scratch_shapes=[pltpu.VMEM(x.shape, x.dtype) for x in (a, dq, dk, dv, g, keys, k_gain) + outs[2:]]
        + [pltpu.SemaphoreType.DMA((11, 2, PIECES))],
        compiler_params=pltpu.CompilerParams(vmem_limit_bytes=LIMIT),
        cost_estimate=pl.CostEstimate(flops=0, bytes_accessed=8 << 20, transcendentals=0),
    )(a, dq, dk, dv, g, keys, k_gain)


def make_table(rows, cols, per, lists):
    _, z, c = place(cols)
    steps = cols * per
    here = lax.dynamic_slice_in_dim(lists, z * steps, steps, 0)[:, WINDOW + GLOBALS :]
    randoms = here.shape[1]
    here = here.reshape(-1)
    place_of = jnp.arange(here.shape[0], dtype=jnp.int32)
    block, slot = place_of // randoms, place_of % randoms
    turn = (STRIDE * (block // per - c + cols) - 1) % cols
    order = (turn * per + block % per) * randoms + slot + 1
    same = (here[:, None] == here[None, :]) & (order[None, :] < order[:, None])
    prev = jnp.max(jnp.where(same, order[None, :], 0), axis=1)
    ids = jnp.arange(lists.shape[0], dtype=jnp.int32)
    last = jnp.max(jnp.where(ids[:, None] == here[None, :], order[None, :], 0), axis=1)
    return jnp.concatenate([here, prev, last]).astype(jnp.int32)


def on_device(depth, queries, keys, values, grad_out, q_gain, k_gain, block_lists):
    cols = k_gain.shape[0]
    rows = lax.axis_size("seq") // cols
    _, tok, wide = queries.shape
    head = q_gain.shape[1]
    width = wide // cols
    heads = width // head
    group = cols * tok
    steps = group // BLOCK
    lists = block_lists[0]
    randoms = lists.shape[1] - WINDOW - GLOBALS
    table = make_table(rows, cols, tok // BLOCK, lists)
    low, full = jnp.bfloat16, jnp.float32
    sem = pltpu.SemaphoreType.DMA
    ring = (rows // 2, 4 * SUBS)
    tile = 2 * heads
    flops = 6 * 2 * group * heads * lists.shape[1] * BLOCK * head
    a, dq, dk, dv, g = pl.pallas_call(
        functools.partial(kernel, rows, cols, depth, randoms),
        out_shape=(
            jax.ShapeDtypeStruct((tok, wide), low),
            jax.ShapeDtypeStruct((tok, wide), low),
            jax.ShapeDtypeStruct((cols, tok, head), low),
            jax.ShapeDtypeStruct((cols, tok, head), low),
            jax.ShapeDtypeStruct((cols, tile, head), full),
        ),
        in_specs=[pl.BlockSpec(memory_space=pltpu.SMEM)] + [ANY] * 4 + [VMEM] * 2,
        out_specs=(ANY,) * 5,
        scratch_shapes=[
            pltpu.VMEM((group, width), low),
            pltpu.VMEM((group, width), low),
            pltpu.VMEM((group, head), low),
            pltpu.VMEM((rows * steps, BLOCK, head), low),
            pltpu.VMEM((rows * steps, BLOCK, head), low),
            pltpu.VMEM((8, head), full),
            pltpu.VMEM((cols, 8, head), full),
            pltpu.VMEM((cols, head), full),
            pltpu.VMEM((cols, head), full),
            pltpu.VMEM((steps, heads * BLOCK, head), low),
            pltpu.VMEM((steps, heads * BLOCK, lists.shape[1] * BLOCK), low),
            pltpu.VMEM((rows * group, head), full),
            pltpu.VMEM((rows * group, head), full),
            pltpu.VMEM((steps * randoms + 1, BLOCK, head), full),
            pltpu.VMEM((steps * randoms + 1, BLOCK, head), full),
            pltpu.VMEM((heads, head), full),
            pltpu.VMEM((1, head), full),
            pltpu.VMEM((steps, heads * BLOCK, 1), full),
            pltpu.VMEM((group, width), low),
            pltpu.VMEM((group, width), low),
            pltpu.VMEM((2, rows // 2 + 1, group, head), low),
            pltpu.VMEM((2, rows // 2 + 1, group, head), low),
            pltpu.VMEM((group, head), low),
            pltpu.VMEM((group, head), low),
            pltpu.VMEM((rows, tile, head), full),
            pltpu.VMEM((depth, tile, head), full),
            pltpu.VMEM((tile, head), full),
            sem((9,)),
            sem((2, cols)),
            sem((2, cols)),
            sem((2, cols)),
            sem((2, cols)),
            sem((cols,)),
            sem((cols,)),
            sem(ring),
            sem(ring),
            sem(ring),
            sem(ring),
            sem((rows,)),
            sem((rows,)),
            sem((2, cols)),
            sem((2, cols)),
            sem(ring),
            sem(ring),
            sem(ring),
            sem(ring),
            sem((2, cols)),
            sem((2, cols)),
            sem((rows,)),
            sem((rows,)),
            sem((depth,)),
            sem((depth,)),
            sem((cols,)),
            sem((cols,)),
        ],
        compiler_params=pltpu.CompilerParams(
            collective_id=0, has_side_effects=True, vmem_limit_bytes=LIMIT
        ),
        cost_estimate=pl.CostEstimate(flops=flops, bytes_accessed=16 << 20, transcendentals=0),
    )(
        table,
        queries[0],
        grad_out[0],
        keys[0],
        values.reshape(tok // BLOCK, BLOCK, head * cols),
        q_gain,
        k_gain,
    )
    a, dq, dk, dv, gain_q, gain_k = finalize(cols, a, dq, dk, dv, g, keys[0], k_gain)
    return a[None], dq[None], dk[None], dv[None], gain_q, gain_k


def solution(mesh):
    spec = P("dp", "seq", None)
    return jax.shard_map(
        functools.partial(on_device, mesh.shape["dp"]),
        mesh=mesh,
        in_specs=(spec, spec, spec, spec, P("seq", None), P(), P("dp", None, None)),
        out_specs=(spec, spec, spec, spec, P("seq", None), P()),
        check_vma=False,
    )
```
